256 devices in a mesh: row: 4 (over z_hi), col: 8 (over y, z_lo), depth: 8 (over x, core).
Axes of the slice: x: 4, y: 4, z: 8 (z_hi: 4, z_lo: 2; z = z_hi * 2 + z_lo), core: 2. Of those that a mesh axis runs over, the one named last changes fastest.
Arguments:
- tokens: bfloat16 [4096, 6144], P(('depth', 'col'), 'row'), may hold values from -20 to 20
- projection_weight: bfloat16 [6144, 24576], P('row', 'col'), may hold values from -0.078125 to 0.078125
- projection_bias: bfloat16 [24576], P('col'), may hold values from -3 to 3
- layer_norm_gain: bfloat16 [6144], P('row'), may hold values from 0.5 to 1.5
- layer_norm_shift: bfloat16 [6144], P('row'), may hold values from -2 to 2
- adapter_down_weight: float32 [32, 6144], P(None, ('row', 'depth')), may hold values from -0.078125 to 0.078125
- adapter_up_weight: float32 [32, 24576], P(None, ('col', 'depth')), may hold values from -0.3 to 0.3
- down_first_moment: float32 [32, 6144], P(None, ('row', 'depth')), may hold values from -300 to 300
- down_second_moment: float32 [32, 6144], P(None, ('row', 'depth')), may hold values from 100 to 10000
- up_first_moment: float32 [32, 24576], P(None, ('col', 'depth')), may hold values from -60 to 60
- up_second_moment: float32 [32, 24576], P(None, ('col', 'depth')), may hold values from 10 to 1000
- cotangent: bfloat16 [4096, 24576], P(('depth', 'row'), 'col'), may hold values from -6 to 6
Outputs:
- hidden: bfloat16 [4096, 24576], P(('depth', 'row'), 'col')
- input_grad: bfloat16 [4096, 6144], P(('depth', 'col'), 'row')
- fresh_down_weight: float32 [32, 6144], P(None, ('row', 'depth'))
- fresh_down_first_moment: float32 [32, 6144], P(None, ('row', 'depth'))
- fresh_down_second_moment: float32 [32, 6144], P(None, ('row', 'depth'))
- fresh_up_weight: float32 [32, 24576], P(None, ('col', 'depth'))
- fresh_up_first_moment: float32 [32, 24576], P(None, ('col', 'depth'))
- fresh_up_second_moment: float32 [32, 24576], P(None, ('col', 'depth'))
The draws below stay inside these ranges and needn't reach their ends.
All inputs are finite; a program needn't handle non-finite values.
Results may differ from the reference program's by a relative error of at most 0.002.
The reference program's roundings to bfloat16 on the way count: a program that leaves them out, or rounds other values in their place, can miss the bound.
Values may be sent and summed in bfloat16 or wider, within the bound.
A program may use at most 128 MiB of HBM per device.

```python
import math
import jax
import jax.numpy as jnp
from jax import lax

MODEL_WIDTH = 6144
HIDDEN_UNITS = 24576
ADAPTER_RANK = 32
SLICE_TOK = 512
TOKENS = 4096
N_DEPTH = 8


def draw_tokens(key, part):
    key = jax.random.fold_in(key, 11)
    first_key, second_key = jax.random.split(key)
    position = jnp.arange(MODEL_WIDTH, dtype=jnp.float32) / (MODEL_WIDTH - 1)
    spread = jnp.power(3.0, position)
    noise = jax.random.normal(first_key, (TOKENS, MODEL_WIDTH), jnp.float32)
    offset = 0.5 * jax.random.normal(second_key, (TOKENS, 1), jnp.float32)
    values = spread[None, :] * (noise + offset)
    return jnp.clip(values, -20.0, 20.0).astype(jnp.bfloat16)


def block_levels(key, extent, shards, smallest, top_value):
    level = 1.0
    for dim, blocks in shards:
        heights = jax.random.uniform(jax.random.fold_in(jax.random.fold_in(key, 6), dim), (blocks,), jnp.float32, smallest / len(shards), top_value / len(shards))
        level = level * jnp.repeat(jnp.exp(heights), extent[dim] // blocks).reshape((-1,) + (1,) * (len(extent) - 1 - dim))
    return level


def gaussian(stream_key, dims, deviation, bound, pieces=(), kind=jnp.bfloat16):
    loudness = block_levels(stream_key, dims, pieces, -0.22, 0.18) if pieces else 1.0
    values = jax.random.normal(stream_key, dims, jnp.float32) * deviation * loudness
    return jnp.minimum(jnp.maximum(values, -bound), bound).astype(kind)


def setup_inputs(seed: int = 0) -> dict:
    arg_keys = jax.random.split(jax.random.key(seed), 13)
    return {
        "tokens": draw_tokens(jax.random.fold_in(arg_keys[12], 71), 0),
        "projection_weight": gaussian(arg_keys[1], (MODEL_WIDTH, HIDDEN_UNITS), MODEL_WIDTH ** -0.5, 0.078125, ((0, 4), (1, 8))),
        "projection_bias": gaussian(arg_keys[2], (HIDDEN_UNITS,), 0.5, 3.0, ((0, 8),)),
        "layer_norm_gain": jnp.clip(1.0 + 0.1 * jax.random.normal(arg_keys[3], (MODEL_WIDTH,), jnp.float32), 0.5, 1.5).astype(jnp.bfloat16),
        "layer_norm_shift": gaussian(arg_keys[4], (MODEL_WIDTH,), 0.3, 2.0, ((0, 4),)),
        "adapter_down_weight": gaussian(arg_keys[5], (ADAPTER_RANK, MODEL_WIDTH), MODEL_WIDTH ** -0.5, 0.078125, ((1, 32),), jnp.float32),
        "adapter_up_weight": gaussian(arg_keys[6], (ADAPTER_RANK, HIDDEN_UNITS), 0.05, 0.3, ((1, 64),), jnp.float32),
        "down_first_moment": gaussian(arg_keys[7], (ADAPTER_RANK, MODEL_WIDTH), 50.0, 300.0, ((1, 32),), jnp.float32),
        "down_second_moment": jnp.clip(jnp.exp(math.log(10000.0) - 4.6051702 * jax.random.uniform(arg_keys[8], (ADAPTER_RANK, MODEL_WIDTH), jnp.float32) ** block_levels(arg_keys[8], (ADAPTER_RANK, MODEL_WIDTH), ((1, 32),), -0.2, 0.2)), 100.0, 10000.0),
        "up_first_moment": gaussian(arg_keys[9], (ADAPTER_RANK, HIDDEN_UNITS), 10.0, 60.0, ((1, 64),), jnp.float32),
        "up_second_moment": jnp.clip(jnp.exp(math.log(1000.0) - 4.6051702 * jax.random.uniform(arg_keys[10], (ADAPTER_RANK, HIDDEN_UNITS), jnp.float32) ** block_levels(arg_keys[10], (ADAPTER_RANK, HIDDEN_UNITS), ((1, 64),), -0.2, 0.2)), 10.0, 1000.0),
        "cotangent": gaussian(arg_keys[11], (TOKENS, HIDDEN_UNITS), 1.0, 6.0, ((0, 32), (1, 8))),
    }


adapter_scale = 0.5
norm_epsilon = 1e-05
beta_first = 0.9
beta_second = 0.999
adam_step = 10
learn_rate = 0.01
decay_rate = 0.1
adam_epsilon = 1e-08

def gelu_slope(values):
    inner = 0.7978845608 * (values + 0.044715 * values * values * values)
    tangent = jnp.tanh(inner)
    return 0.5 * (1.0 + tangent) + 0.5 * values * (1.0 - tangent * tangent) * 0.7978845608 * (1.0 + 3.0 * 0.044715 * values * values)

def decoupled_adam_update(weights_now, moment, square, gradient):
    new_moment = beta_first * moment + (1.0 - beta_first) * gradient
    new_square = beta_second * square + (1.0 - beta_second) * gradient * gradient
    update = new_moment / (1.0 - beta_first ** adam_step) / (jnp.sqrt(new_square / (1.0 - beta_second ** adam_step)) + adam_epsilon)
    return (weights_now - learn_rate * (update + decay_rate * weights_now), new_moment, new_square)

def reference(tokens, projection_weight, projection_bias, layer_norm_gain, layer_norm_shift, adapter_down_weight, adapter_up_weight, down_first_moment, down_second_moment, up_first_moment, up_second_moment, cotangent):
    down_partial = adapter_down_weight.astype(jnp.bfloat16)
    up_partial = adapter_up_weight.astype(jnp.bfloat16)
    highest_precision = lax.Precision.HIGHEST
    token_slices = tokens.reshape(N_DEPTH, SLICE_TOK, MODEL_WIDTH)
    cot_slices = cotangent.reshape(N_DEPTH, SLICE_TOK, HIDDEN_UNITS)

    def one_slice(carry_state, paired):
        token_rows, cot_rows = paired
        values = token_rows.astype(jnp.float32)
        mean_value = lax.optimization_barrier(jnp.mean(values, axis=1, keepdims=True))
        mean_square = lax.optimization_barrier(jnp.mean(values * values, axis=1, keepdims=True))
        inv_std = lax.rsqrt(mean_square - mean_value * mean_value + norm_epsilon)
        centred = (values - mean_value) * inv_std
        normalized_input = (centred * layer_norm_gain + layer_norm_shift).astype(jnp.bfloat16)
        rank_projection = lax.dot_general(normalized_input, down_partial, (((1,), (1,)), ((), ())), preferred_element_type=jnp.float32)
        preactivation_value = jnp.dot(normalized_input, projection_weight, preferred_element_type=jnp.float32) + projection_bias + adapter_scale * jnp.dot(rank_projection, adapter_up_weight, precision=highest_precision)
        hidden = jax.nn.gelu(preactivation_value, approximate=True).astype(jnp.bfloat16)
        activation_slopes = (cot_rows.astype(jnp.float32) * gelu_slope(preactivation_value)).astype(jnp.bfloat16)
        adapter_backward = lax.dot_general(activation_slopes, up_partial, (((1,), (1,)), ((), ())), preferred_element_type=jnp.float32)
        normalized_gradient = lax.dot_general(activation_slopes, projection_weight, (((1,), (1,)), ((), ())), preferred_element_type=jnp.float32) + adapter_scale * jnp.dot(adapter_backward, adapter_down_weight, precision=highest_precision)
        scaled = normalized_gradient * layer_norm_gain
        input_grad = (inv_std * (scaled - lax.optimization_barrier(jnp.mean(scaled, axis=1, keepdims=True)) - centred * lax.optimization_barrier(jnp.mean(scaled * centred, axis=1, keepdims=True)))).astype(jnp.bfloat16)
        up_gradient_sum = carry_state[0] + adapter_scale * jnp.dot(rank_projection.T, activation_slopes.astype(jnp.float32), precision=highest_precision)
        down_gradient_sum = carry_state[1] + adapter_scale * jnp.dot(adapter_backward.T, normalized_input.astype(jnp.float32), precision=highest_precision)
        return ((up_gradient_sum, down_gradient_sum), (hidden, input_grad))
    start_grads = (jnp.zeros((ADAPTER_RANK, HIDDEN_UNITS), jnp.float32), jnp.zeros((ADAPTER_RANK, MODEL_WIDTH), jnp.float32))
    gradient_pair, outputs = lax.scan(one_slice, start_grads, (token_slices, cot_slices))
    hidden = outputs[0].reshape(TOKENS, HIDDEN_UNITS)
    input_grad = outputs[1].reshape(TOKENS, MODEL_WIDTH)
    fresh_down_weight, fresh_down_first_moment, fresh_down_second_moment = decoupled_adam_update(adapter_down_weight, down_first_moment, down_second_moment, gradient_pair[1])
    fresh_up_weight, fresh_up_first_moment, fresh_up_second_moment = decoupled_adam_update(adapter_up_weight, up_first_moment, up_second_moment, gradient_pair[0])
    return (hidden, input_grad, fresh_down_weight, fresh_down_first_moment, fresh_down_second_moment, fresh_up_weight, fresh_up_first_moment, fresh_up_second_moment)
```

```python
import functools
import jax
import jax.numpy as jnp
from jax import lax
from jax.experimental import pallas as pl
from jax.experimental.pallas import tpu as pltpu
from jax.sharding import PartitionSpec as P

adapter_scale = 0.5
norm_epsilon = 1e-05
beta_first = 0.9
beta_second = 0.999
adam_step = 10
learn_rate = 0.01
decay_rate = 0.1
adam_epsilon = 1e-08

f32 = jnp.float32
bf16 = jnp.bfloat16
MESH = pl.DeviceIdType.MESH
NT = (((1,), (1,)), ((), ()))

ROWS, COLS, DEPTH = 4, 8, 8
YS = COLS // 2
CHUNKS = 4
OWN = 64
STEP = OWN // CHUNKS
TOK = STEP * COLS
FEAT, HID, RANK = 1536, 3072, 32
UPB, DNB = HID // DEPTH, FEAT // DEPTH
RING = 2 * STEP
CODE_SPAN = 120.0
LN2 = 0.6931471805599453
TILE = 512


def gelu_both(v):
    inner = 0.7978845608 * (v + 0.044715 * v * v * v)
    tangent = jnp.tanh(inner)
    value = 0.5 * v * (1.0 + tangent)
    slope = 0.5 * (1.0 + tangent) + 0.5 * v * (1.0 - tangent * tangent) * 0.7978845608 * (
        1.0 + 3.0 * 0.044715 * v * v
    )
    return value, slope


def adam(weight, moment, square, gradient):
    new_moment = beta_first * moment + (1.0 - beta_first) * gradient
    new_square = beta_second * square + (1.0 - beta_second) * gradient * gradient
    update = (
        new_moment
        / (1.0 - beta_first**adam_step)
        / (jnp.sqrt(new_square / (1.0 - beta_second**adam_step)) + adam_epsilon)
    )
    return weight - learn_rate * (update + decay_rate * weight), new_moment, new_square


def encode(load, store, rows, width):
    top = jnp.zeros((rows, 1), f32)
    for t in range(0, width, TILE):
        top = jnp.maximum(top, jnp.max(jnp.abs(load(t)), axis=1, keepdims=True))
    top = (jnp.maximum(top, 1e-30) * 1.01).astype(bf16)
    factor = CODE_SPAN / top.astype(f32)
    for t in range(0, width, TILE):
        store(t, TILE, jnp.exp2(load(t) * factor).astype(bf16))
    store(width, 128, jnp.broadcast_to(top, (rows, 128)))


def decoder(load, width):
    scale = load(width, 128)[:, 0:1].astype(f32) * (1.0 / (CODE_SPAN * LN2))
    return lambda t: jnp.log(load(t, TILE).astype(f32)) * scale


def kernel(
    tok,
    w_hbm,
    bias,
    gain,
    shift,
    down_w,
    up_w,
    down_m,
    down_s,
    up_m,
    up_s,
    cot_hbm,
    hidden,
    input_grad,
    new_down_w,
    new_down_m,
    new_down_s,
    new_up_w,
    new_up_m,
    new_up_s,
    w,
    cot,
    local_sem,
    stat_s,
    stat_r,
    cen,
    istd,
    nrm,
    upg,
    dng,
    d_low,
    d_prod,
    u_low,
    u_prod,
    part,
    low,
    rs_s,
    rs_r,
    slg,
    back,
    cs_s,
    cs_r,
    lo_s,
    lo_r,
    ng,
    gst_s,
    gst_r,
    up_acc,
    dn_acc,
    ugs,
    ugr,
    dgs,
    dgr,
    upx,
    dnx,
    stat_sem,
    nlo_sem,
    nown_sem,
    nfwd_sem,
    upg_sem,
    dng_sem,
    rs_sem,
    ag_sem,
    cs_sem,
    lo_sem,
    gst_sem,
    ug_sem,
    dg_sem,
    ux_sem,
    dx_sem,
):
    r = lax.axis_index("row")
    c = lax.axis_index("col")
    d = lax.axis_index("depth")
    y, lo = c // 2, c % 2
    right, left, opp = (r + 1) % ROWS, (r + 3) % ROWS, (r + 2) % ROWS
    pc = y * 2 + (1 - lo)

    def remote(src, dst, sems, index, device):
        return pltpu.make_async_remote_copy(
            src_ref=src,
            dst_ref=dst,
            send_sem=sems.at[(0,) + index],
            recv_sem=sems.at[(1,) + index],
            device_id=device,
            device_id_type=MESH,
        )

    w_copy = pltpu.make_async_copy(w_hbm, w, local_sem.at[0])
    cot_copy = pltpu.make_async_copy(cot_hbm, cot, local_sem.at[1])
    w_copy.start()
    cot_copy.start()

    barrier = pltpu.get_barrier_semaphore()
    for j in range(1, ROWS):
        pl.semaphore_signal(barrier, inc=1, device_id={"row": (r + j) % ROWS}, device_id_type=MESH)
    for j in range(1, COLS):
        pl.semaphore_signal(barrier, inc=1, device_id={"col": (c + j) % COLS}, device_id_type=MESH)
    for j in range(1, DEPTH):
        pl.semaphore_signal(
            barrier, inc=1, device_id={"depth": (d + j) % DEPTH}, device_id_type=MESH
        )

    x = tok[...].astype(f32)
    lane = lax.broadcasted_iota(jnp.int32, (OWN, 128), 1)
    s1 = jnp.sum(x, axis=1, keepdims=True)
    s2 = jnp.sum(x * x, axis=1, keepdims=True)
    stat_s[...] = jnp.where(lane == 0, s1, jnp.where(lane == 1, s2, 0.0))
    upg[d] = up_w[...]
    dng[d] = down_w[...]
    pl.semaphore_wait(barrier, ROWS + COLS + DEPTH - 3)

    def stat_copy(j):
        return remote(stat_s, stat_r.at[j - 1], stat_sem, (j,), {"row": (r + j) % ROWS})

    def upg_copy(j, owner):
        return remote(upg.at[owner], upg.at[owner], upg_sem, (j,), {"depth": (d + j) % DEPTH})

    def dng_copy(j, owner):
        return remote(dng.at[owner], dng.at[owner], dng_sem, (j,), {"depth": (d + j) % DEPTH})

    for j in range(1, ROWS):
        stat_copy(j).start()
    for j in range(1, DEPTH):
        dng_copy(j, d).start()
        upg_copy(j, d).start()
    for j in range(1, ROWS):
        stat_copy(j).wait_recv()
    total = stat_s[...] + stat_r[0] + stat_r[1] + stat_r[2]
    count = 1.0 / (FEAT * ROWS)
    mean = total[:, 0:1] * count
    inv = lax.rsqrt(total[:, 1:2] * count - mean * mean + norm_epsilon)
    istd[...] = jnp.broadcast_to(inv, (OWN, 128))
    centred = (x - mean) * inv
    cen[...] = centred
    normed = (centred * gain[...].astype(f32) + shift[...].astype(f32)).astype(bf16)
    for k in range(CHUNKS):
        nrm[k, pl.ds(pl.multiple_of(STEP * c, STEP), STEP), :] = normed[STEP * k : STEP * (k + 1)]

    def token_rows(k, col):
        return nrm.at[k, pl.ds(pl.multiple_of(STEP * col, STEP), STEP)]

    def nlo_copy(k, col):
        return remote(token_rows(k, col), token_rows(k, col), nlo_sem, (k,), {"col": pc})

    def y_peer(j):
        return {"col": ((y + j) % YS) * 2 + lo}

    def nown_copy(k, j, col):
        return remote(token_rows(k, col), token_rows(k, col), nown_sem, (k, j), y_peer(j))

    def nfwd_copy(k, j, col):
        return remote(token_rows(k, col), token_rows(k, col), nfwd_sem, (k, j), y_peer(j))

    def send_own(k, carry):
        nlo_copy(k, c).start()
        for j in range(1, YS):
            nown_copy(k, j, c).start()
        return carry

    lax.fori_loop(0, CHUNKS, send_own, 0)

    def forward_tokens(k):
        nlo_copy(k, pc).wait_recv()
        for j in range(1, YS):
            nfwd_copy(k, j, pc).start()

    forward_tokens(0)

    for j in range(1, DEPTH):
        owner = (d + DEPTH - j) % DEPTH
        dng_copy(j, owner).wait_recv()
        upg_copy(j, owner).wait_recv()
    for i in range(DEPTH):
        u = upg[i]
        high = u.astype(bf16)
        mid_part = (u - high.astype(f32)).astype(bf16)
        zero = jnp.zeros_like(high)
        cols = slice(UPB * i, UPB * (i + 1))
        u_low[:, cols] = jnp.concatenate([high, high, high, zero], axis=0)
        u_prod[:, cols] = jnp.concatenate([high, mid_part, high, zero], axis=0)
    for i in range(DEPTH // 2):
        u = jnp.concatenate([dng[2 * i], dng[2 * i + 1]], axis=1)
        high = u.astype(bf16)
        mid_part = (u - high.astype(f32)).astype(bf16)
        zero = jnp.zeros_like(high)
        cols = slice(2 * DNB * i, 2 * DNB * (i + 1))
        d_low[:, cols] = jnp.concatenate([high, high, high, zero], axis=0)
        d_prod[:, cols] = jnp.concatenate([high, mid_part, high, zero], axis=0)
    up_acc[...] = jnp.zeros_like(up_acc)
    dn_acc[...] = jnp.zeros_like(dn_acc)
    w_copy.wait()
    cot_copy.wait()

    def split(value):
        high = value.astype(bf16).astype(f32)
        lanes = lax.broadcasted_iota(jnp.int32, value.shape, 1)
        return jnp.where(lanes < 2 * RANK, high, value - high).astype(bf16)

    def part_rows(k, owner, half):
        start = pl.multiple_of(RING * owner + STEP * half, STEP)
        return k, pl.ds(start, STEP)

    def rs_copy(k, slot):
        target = right if slot < 3 else left
        return remote(rs_s.at[k, slot], rs_r.at[k, slot], rs_sem, (k, slot), {"row": target})

    def rs_decoder(k, slot):
        return decoder(lambda t, n: rs_r[k, slot, :, t : t + n], HID)

    def rs_send(k, slot, owner, half):
        kk, rows = part_rows(k, owner, half)

        def store(t, n, value):
            rs_s[k, slot, :, t : t + n] = value

        encode(lambda t: part[kk, rows, t : t + TILE], store, STEP, HID)
        rs_copy(k, slot).start()

    def phase_forward(k):
        for j in range(1, YS):
            source = (y + YS - j) % YS
            nown_copy(k, j, source * 2 + lo).wait_recv()
            nfwd_copy(k, j, source * 2 + (1 - lo)).wait_recv()
        lhs = nrm[k]
        rank = split(
            adapter_scale
            * lax.dot_general(lhs, d_low[...], NT, preferred_element_type=f32)
        )
        low[k] = rank

        def tile(t, carry):
            cols = pl.ds(pl.multiple_of(t * TILE, TILE), TILE)
            part[k, :, cols] = jnp.dot(
                nrm[k], w[:, cols], preferred_element_type=f32
            ) + jnp.dot(low[k], u_prod[:, cols], preferred_element_type=f32)
            return carry

        lax.fori_loop(0, HID // TILE, tile, 0)
        rs_send(k, 0, opp, 0)
        rs_send(k, 3, opp, 1)
        rs_send(k, 1, right, 1)
        rs_send(k, 4, left, 0)

    def phase_relay(k):
        for slot, owner, half in ((0, right, 0), (3, left, 1)):
            rs_copy(k, slot).wait_recv()
            kk, rows = part_rows(k, owner, half)
            got = rs_decoder(k, slot)
            for t in range(0, HID, TILE):
                part[kk, rows, t : t + TILE] += got(t)
            rs_send(k, slot + 2, owner, half)

    def slope_rows(k, owner, first, count_):
        return slg.at[k, pl.ds(pl.multiple_of(RING * owner + first, STEP), count_)]

    def ag_copy(k, slot, owner):
        rows = (
            slope_rows(k, owner, 0, RING)
            if slot in (0, 2)
            else slope_rows(k, owner, 0 if slot == 1 else STEP, STEP)
        )
        target = right if slot < 2 else left
        return remote(rows, rows, ag_sem, (k, slot), {"row": target})

    def phase_middle(k):
        for half, first, second in ((0, 4, 2), (1, 1, 5)):
            rs_copy(k, first).wait_recv()
            rs_copy(k, second).wait_recv()
            kk, rows = part_rows(k, r, half)
            one, two = rs_decoder(k, first), rs_decoder(k, second)
            start = pl.multiple_of(OWN * half + STEP * k, STEP)
            for t in range(0, HID, TILE):
                cols = slice(t, t + TILE)
                v = part[kk, rows, cols] + one(t) + two(t) + bias[:, cols].astype(f32)
                value, slope = gelu_both(v)
                hidden[pl.ds(start, STEP), cols] = value.astype(bf16)
                slg[kk, rows, cols] = (
                    cot[pl.ds(start, STEP), cols].astype(f32) * slope
                ).astype(bf16)
        ag_copy(k, 0, r).start()
        ag_copy(k, 2, r).start()

    def phase_spread(k):
        ag_copy(k, 0, left).wait_recv()
        ag_copy(k, 1, left).start()
        ag_copy(k, 2, right).wait_recv()
        ag_copy(k, 3, right).start()

    def cs_copy(k, j):
        return remote(cs_s.at[k, j - 1], cs_r.at[k, j - 1], cs_sem, (k, j), y_peer(j))

    def phase_backward(k):
        ag_copy(k, 1, opp).wait_recv()
        ag_copy(k, 3, opp).wait_recv()
        slopes = slg[k]
        rank = split(
            adapter_scale * lax.dot_general(slopes, u_low[...], NT, preferred_element_type=f32)
        )
        bsize = 256

        def tile(t, carry):
            rows = pl.ds(pl.multiple_of(t * bsize, bsize), bsize)
            back[k, :, rows] = lax.dot_general(
                slg[k], w[rows, :], NT, preferred_element_type=f32
            ) + jnp.dot(rank, d_prod[:, rows], preferred_element_type=f32)
            return carry

        lax.fori_loop(0, FEAT // bsize, tile, 0)
        for j in range(1, YS):
            rows = pl.ds(pl.multiple_of(RING * ((y + j) % YS), RING), RING)

            def store(t, n, value):
                cs_s[k, j - 1, :, t : t + n] = value

            encode(lambda t: back[k, rows, t : t + TILE], store, RING, FEAT)
            cs_copy(k, j).start()
        low_t = low[k].astype(f32).T.astype(bf16)
        rank_t = rank.astype(f32).T.astype(bf16)

        def grow(t, carry):
            cols = pl.ds(pl.multiple_of(t * TILE, TILE), TILE)
            g = jnp.dot(low_t, slg[k, :, cols], preferred_element_type=f32)
            up_acc[:, cols] += g[0:RANK] + g[2 * RANK : 3 * RANK]
            return carry

        lax.fori_loop(0, HID // TILE, grow, 0)

        def grow_down(t, carry):
            cols = pl.ds(pl.multiple_of(t * TILE, TILE), TILE)
            g = jnp.dot(rank_t, nrm[k, :, cols], preferred_element_type=f32)
            dn_acc[:, cols] += g[0:RANK] + g[2 * RANK : 3 * RANK]
            return carry

        lax.fori_loop(0, FEAT // TILE, grow_down, 0)

    def lo_copy(k):
        return remote(lo_s.at[k], lo_r.at[k], lo_sem, (k,), {"col": pc})

    def phase_fold(k):
        mine = pl.ds(pl.multiple_of(RING * y, RING), RING)
        for j in range(1, YS):
            cs_copy(k, j).wait_recv()
            got = decoder(lambda t, n: cs_r[k, j - 1, :, t : t + n], FEAT)
            for t in range(0, FEAT, TILE):
                back[k, mine, t : t + TILE] += got(t)
        other = pl.ds(pl.multiple_of(RING * y + STEP * (1 - lo), STEP), STEP)

        def store(t, n, value):
            lo_s[k, :, t : t + n] = value

        encode(lambda t: back[k, other, t : t + TILE], store, STEP, FEAT)
        lo_copy(k).start()

    def gst_copy(k, j):
        return remote(gst_s.at[k], gst_r.at[k, j - 1], gst_sem, (k, j), {"row": (r + j) % ROWS})

    def own_rows(k):
        return pl.ds(pl.multiple_of(STEP * k, STEP), STEP)

    def phase_stats(k):
        lo_copy(k).wait_recv()
        mine = pl.ds(pl.multiple_of(RING * y + STEP * lo, STEP), STEP)
        got = decoder(lambda t, n: lo_r[k, :, t : t + n], FEAT)
        one = jnp.zeros((STEP, 1), f32)
        two = jnp.zeros((STEP, 1), f32)
        for t in range(0, FEAT, TILE):
            cols = slice(t, t + TILE)
            scaled = (back[k, mine, cols] + got(t)) * gain[:, cols].astype(f32)
            ng[k, :, cols] = scaled
            one += jnp.sum(scaled, axis=1, keepdims=True)
            two += jnp.sum(scaled * cen[own_rows(k), cols], axis=1, keepdims=True)
        lanes = lax.broadcasted_iota(jnp.int32, (STEP, 128), 1)
        gst_s[k] = jnp.where(lanes == 0, one, jnp.where(lanes == 1, two, 0.0))
        for j in range(1, ROWS):
            gst_copy(k, j).start()

    def phase_finish(k):
        for j in range(1, ROWS):
            gst_copy(k, j).wait_recv()
        sums = (gst_s[k] + gst_r[k, 0] + gst_r[k, 1] + gst_r[k, 2]) * count
        inv_ = istd[own_rows(k), 0:1]
        for t in range(0, FEAT, TILE):
            cols = slice(t, t + TILE)
            input_grad[own_rows(k), cols] = (
                inv_ * (ng[k, :, cols] - sums[:, 0:1] - cen[own_rows(k), cols] * sums[:, 1:2])
            ).astype(bf16)

    def ug_copy(j):
        peer = (d + j) % DEPTH
        return remote(ugs.at[peer], ugr.at[j], ug_sem, (j,), {"depth": peer})

    def dg_copy(j):
        peer = (d + j) % DEPTH
        return remote(dgs.at[peer], dgr.at[j], dg_sem, (j,), {"depth": peer})

    def ux_copy(j, owner):
        return remote(upx.at[owner], upx.at[owner], ux_sem, (j,), {"row": (r + j) % ROWS})

    def dx_copy(j, owner):
        return remote(dnx.at[owner], dnx.at[owner], dx_sem, (j,), {"col": (c + j) % COLS})

    def grads_send():
        for i in range(DEPTH):
            ugs[i] = up_acc[:, UPB * i : UPB * (i + 1)]
            dgs[i] = dn_acc[:, DNB * i : DNB * (i + 1)]
        for j in range(1, DEPTH):
            ug_copy(j).start()
            dg_copy(j).start()

    def grads_spread():
        up_sum = ugs[d]
        dn_sum = dgs[d]
        for j in range(1, DEPTH):
            ug_copy(j).wait_recv()
            dg_copy(j).wait_recv()
            up_sum += ugr[j]
            dn_sum += dgr[j]
        upx[r] = up_sum
        dnx[c] = dn_sum
        for j in range(1, ROWS):
            ux_copy(j, r).start()
        for j in range(1, COLS):
            dx_copy(j, c).start()

    def iteration(it, carry):
        @pl.when(it < CHUNKS)
        def _():
            phase_forward(it)

        @pl.when(it < CHUNKS - 1)
        def _():
            forward_tokens(it + 1)

        @pl.when(it < CHUNKS)
        def _():
            phase_relay(it)

        @pl.when((it >= 3) & (it < CHUNKS + 3))
        def _():
            phase_backward(it - 3)

        @pl.when(it == CHUNKS + 2)
        def _():
            grads_send()

        @pl.when((it >= 2) & (it < CHUNKS + 2))
        def _():
            phase_spread(it - 2)

        @pl.when((it >= 1) & (it < CHUNKS + 1))
        def _():
            phase_middle(it - 1)

        @pl.when((it >= 4) & (it < CHUNKS + 4))
        def _():
            phase_fold(it - 4)

        @pl.when(it == CHUNKS + 3)
        def _():
            grads_spread()

        @pl.when((it >= 5) & (it < CHUNKS + 5))
        def _():
            phase_stats(it - 5)

        @pl.when(it >= 6)
        def _():
            phase_finish(it - 6)

        return carry

    lax.fori_loop(0, CHUNKS + 6, iteration, 0)

    for j in range(1, ROWS):
        ux_copy(j, (r + ROWS - j) % ROWS).wait_recv()
    for j in range(1, COLS):
        dx_copy(j, (c + COLS - j) % COLS).wait_recv()
    up_gradient = upx[0]
    for i in range(1, ROWS):
        up_gradient += upx[i]
    down_gradient = dnx[0]
    for i in range(1, COLS):
        down_gradient += dnx[i]
    new_up_w[...], new_up_m[...], new_up_s[...] = adam(up_w[...], up_m[...], up_s[...], up_gradient)
    new_down_w[...], new_down_m[...], new_down_s[...] = adam(
        down_w[...], down_m[...], down_s[...], down_gradient
    )

    for j in range(1, ROWS):
        stat_copy(j).wait_send()
        ux_copy(j, r).wait_send()
    for j in range(1, COLS):
        dx_copy(j, c).wait_send()
    for j in range(1, DEPTH):
        dng_copy(j, d).wait_send()
        upg_copy(j, d).wait_send()
        ug_copy(j).wait_send()
        dg_copy(j).wait_send()

    def drain(k, carry):
        nlo_copy(k, c).wait_send()
        for j in range(1, YS):
            nown_copy(k, j, c).wait_send()
            nfwd_copy(k, j, pc).wait_send()
            cs_copy(k, j).wait_send()
        for slot in range(6):
            rs_copy(k, slot).wait_send()
        for slot, owner in ((0, r), (1, left), (2, r), (3, right)):
            ag_copy(k, slot, owner).wait_send()
        lo_copy(k).wait_send()
        for j in range(1, ROWS):
            gst_copy(k, j).wait_send()
        return carry

    lax.fori_loop(0, CHUNKS, drain, 0)


def shards(*blocks):
    (tok, w, bias, gain, shift, down_w, up_w, down_m, down_s, up_m, up_s, cot) = blocks
    vmem = pl.BlockSpec(memory_space=pltpu.VMEM)
    hbm = pl.BlockSpec(memory_space=pl.ANY)
    n = CHUNKS
    dma = pltpu.SemaphoreType.DMA
    small = jax.ShapeDtypeStruct((RANK, DNB), f32)
    wide = jax.ShapeDtypeStruct((RANK, UPB), f32)
    scratch = [
        pltpu.VMEM((FEAT, HID), bf16),
        pltpu.VMEM((2 * OWN, HID), bf16),
        dma((2,)),
        pltpu.VMEM((OWN, 128), f32),
        pltpu.VMEM((ROWS - 1, OWN, 128), f32),
        pltpu.VMEM((OWN, FEAT), f32),
        pltpu.VMEM((OWN, 128), f32),
        pltpu.VMEM((n, TOK, FEAT), bf16),
        pltpu.VMEM((DEPTH, RANK, UPB), f32),
        pltpu.VMEM((DEPTH, RANK, DNB), f32),
        pltpu.VMEM((4 * RANK, FEAT), bf16),
        pltpu.VMEM((4 * RANK, FEAT), bf16),
        pltpu.VMEM((4 * RANK, HID), bf16),
        pltpu.VMEM((4 * RANK, HID), bf16),
        pltpu.VMEM((n, TOK, HID), f32),
        pltpu.VMEM((n, TOK, 4 * RANK), bf16),
        pltpu.VMEM((n, 6, STEP, HID + 128), bf16),
        pltpu.VMEM((n, 6, STEP, HID + 128), bf16),
        pltpu.VMEM((n, TOK, HID), bf16),
        pltpu.VMEM((n, TOK, FEAT), f32),
        pltpu.VMEM((n, YS - 1, RING, FEAT + 128), bf16),
        pltpu.VMEM((n, YS - 1, RING, FEAT + 128), bf16),
        pltpu.VMEM((n, STEP, FEAT + 128), bf16),
        pltpu.VMEM((n, STEP, FEAT + 128), bf16),
        pltpu.VMEM((n, STEP, FEAT), f32),
        pltpu.VMEM((n, STEP, 128), f32),
        pltpu.VMEM((n, ROWS - 1, STEP, 128), f32),
        pltpu.VMEM((RANK, HID), f32),
        pltpu.VMEM((RANK, FEAT), f32),
        pltpu.VMEM((DEPTH, RANK, UPB), f32),
        pltpu.VMEM((DEPTH, RANK, UPB), f32),
        pltpu.VMEM((DEPTH, RANK, DNB), f32),
        pltpu.VMEM((DEPTH, RANK, DNB), f32),
        pltpu.VMEM((ROWS, RANK, UPB), f32),
        pltpu.VMEM((COLS, RANK, DNB), f32),
        dma((2, ROWS)),
        dma((2, n)),
        dma((2, n, YS)),
        dma((2, n, YS)),
        dma((2, DEPTH)),
        dma((2, DEPTH)),
        dma((2, n, 6)),
        dma((2, n, 4)),
        dma((2, n, YS)),
        dma((2, n)),
        dma((2, n, ROWS)),
        dma((2, DEPTH)),
        dma((2, DEPTH)),
        dma((2, ROWS)),
        dma((2, COLS)),
    ]
    return pl.pallas_call(
        kernel,
        out_shape=(
            jax.ShapeDtypeStruct((2 * OWN, HID), bf16),
            jax.ShapeDtypeStruct((OWN, FEAT), bf16),
            small,
            small,
            small,
            wide,
            wide,
            wide,
        ),
        in_specs=[vmem, hbm] + [vmem] * 9 + [hbm],
        out_specs=(vmem,) * 8,
        scratch_shapes=scratch,
        compiler_params=pltpu.CompilerParams(
            collective_id=0, has_side_effects=True, vmem_limit_bytes=56 * 1024 * 1024
        ),
        cost_estimate=pl.CostEstimate(
            flops=4 * 512 * FEAT * HID, bytes_accessed=14000000, transcendentals=10000000
        ),
        name="fused_step",
    )(
        tok,
        w,
        bias.reshape(1, HID),
        gain.reshape(1, FEAT),
        shift.reshape(1, FEAT),
        down_w,
        up_w,
        down_m,
        down_s,
        up_m,
        up_s,
        cot,
    )


def solution(mesh):
    down = P(None, ("row", "depth"))
    up = P(None, ("col", "depth"))
    return jax.shard_map(
        shards,
        mesh=mesh,
        in_specs=(
            P(("depth", "col"), "row"),
            P("row", "col"),
            P("col"),
            P("row"),
            P("row"),
            down,
            up,
            down,
            down,
            up,
            up,
            P(("depth", "row"), "col"),
        ),
        out_specs=(
            P(("depth", "row"), "col"),
            P(("depth", "col"), "row"),
            down,
            down,
            down,
            up,
            up,
            up,
        ),
        check_vma=False,
    )
```

```python
import functools
import jax
import jax.numpy as jnp
from jax import lax
from jax.experimental import pallas as pl
from jax.experimental.pallas import tpu as pltpu
from jax.sharding import PartitionSpec as P

adapter_scale = 0.5
norm_epsilon = 1e-05
beta_first = 0.9
beta_second = 0.999
adam_step = 10
learn_rate = 0.01
decay_rate = 0.1
adam_epsilon = 1e-08

f32 = jnp.float32
bf16 = jnp.bfloat16
MESH = pl.DeviceIdType.MESH
NT = (((1,), (1,)), ((), ()))

ROWS, COLS, DEPTH = 4, 8, 8
YS = COLS // 2
CHUNKS = 4
OWN = 64
STEP = OWN // CHUNKS
TOK = STEP * COLS
FEAT, HID, RANK = 1536, 3072, 32
UPB, DNB = HID // DEPTH, FEAT // DEPTH
RING = 2 * STEP
CODE_SPAN = 120.0
LN2 = 0.6931471805599453
TILE = 512


def gelu_both(v):
    inner = 0.7978845608 * (v + 0.044715 * v * v * v)
    tangent = jnp.tanh(inner)
    value = 0.5 * v * (1.0 + tangent)
    slope = 0.5 * (1.0 + tangent) + 0.5 * v * (1.0 - tangent * tangent) * 0.7978845608 * (
        1.0 + 3.0 * 0.044715 * v * v
    )
    return value, slope


def adam(weight, moment, square, gradient):
    new_moment = beta_first * moment + (1.0 - beta_first) * gradient
    new_square = beta_second * square + (1.0 - beta_second) * gradient * gradient
    update = (
        new_moment
        / (1.0 - beta_first**adam_step)
        / (jnp.sqrt(new_square / (1.0 - beta_second**adam_step)) + adam_epsilon)
    )
    return weight - learn_rate * (update + decay_rate * weight), new_moment, new_square


def encode(load, store, rows, width):
    top = jnp.zeros((rows, 1), f32)
    for t in range(0, width, TILE):
        top = jnp.maximum(top, jnp.max(jnp.abs(load(t)), axis=1, keepdims=True))
    top = (jnp.maximum(top, 1e-30) * 1.01).astype(bf16)
    factor = CODE_SPAN / top.astype(f32)
    for t in range(0, width, TILE):
        store(t, TILE, jnp.exp2(load(t) * factor).astype(bf16))
    store(width, 128, jnp.broadcast_to(top, (rows, 128)))


def decoder(load, width):
    scale = load(width, 128)[:, 0:1].astype(f32) * (1.0 / (CODE_SPAN * LN2))
    return lambda t: jnp.log(load(t, TILE).astype(f32)) * scale


def kernel(
    tok,
    w_hbm,
    bias,
    gain,
    shift,
    down_w,
    up_w,
    cot_hbm,
    hidden,
    input_grad,
    down_grad,
    up_grad,
    w,
    cot,
    local_sem,
    stat_s,
    stat_r,
    gain_row,
    shift_row,
    bias_row,
    raw,
    mst,
    nrm,
    upg,
    dng,
    d_low,
    d_prod,
    u_low,
    u_prod,
    part,
    low,
    rs_s,
    rs_r,
    slg,
    back,
    cs_s,
    cs_r,
    lo_s,
    lo_r,
    ng,
    gst_s,
    gst_r,
    low_own,
    dn_acc,
    ugs,
    ugr,
    dgs,
    dgr,
    upx,
    dnx,
    stat_sem,
    mst_sem,
    nlo_sem,
    nown_sem,
    nfwd_sem,
    upg_sem,
    dng_sem,
    rs_sem,
    ag_sem,
    cs_sem,
    lo_sem,
    gst_sem,
    ug_sem,
    dg_sem,
    ux_sem,
    dx_sem,
):
    r = lax.axis_index("row")
    c = lax.axis_index("col")
    d = lax.axis_index("depth")
    y, lo = c // 2, c % 2
    right, left, opp = (r + 1) % ROWS, (r + 3) % ROWS, (r + 2) % ROWS
    pc = y * 2 + (1 - lo)

    def remote(src, dst, sems, index, device):
        return pltpu.make_async_remote_copy(
            src_ref=src,
            dst_ref=dst,
            send_sem=sems.at[(0,) + index],
            recv_sem=sems.at[(1,) + index],
            device_id=device,
            device_id_type=MESH,
        )

    w_copy = pltpu.make_async_copy(w_hbm, w, local_sem.at[0])
    cot_copy = pltpu.make_async_copy(cot_hbm, cot, local_sem.at[1])
    w_copy.start()
    cot_copy.start()

    barrier = pltpu.get_barrier_semaphore()
    for j in range(1, ROWS):
        pl.semaphore_signal(barrier, inc=1, device_id={"row": (r + j) % ROWS}, device_id_type=MESH)
    for j in range(1, COLS):
        pl.semaphore_signal(barrier, inc=1, device_id={"col": (c + j) % COLS}, device_id_type=MESH)
    for j in range(1, DEPTH):
        pl.semaphore_signal(
            barrier, inc=1, device_id={"depth": (d + j) % DEPTH}, device_id_type=MESH
        )

    x = tok[...].astype(f32)
    lane = lax.broadcasted_iota(jnp.int32, (OWN, 128), 1)
    s1 = jnp.sum(x, axis=1, keepdims=True)
    s2 = jnp.sum(x * x, axis=1, keepdims=True)
    sums = jnp.where(lane == 0, s1, jnp.where(lane == 1, s2, 0.0))
    stat_s[...] = jnp.concatenate([sums, jnp.zeros_like(sums)], axis=0).T[0:8]
    upg[d] = up_w[...]
    dng[d] = down_w[...]
    for k in range(CHUNKS):
        raw[k, pl.ds(pl.multiple_of(STEP * c, STEP), STEP), :] = tok[STEP * k : STEP * (k + 1), :]
    pl.semaphore_wait(barrier, ROWS + COLS + DEPTH - 3)

    def stat_copy(j):
        return remote(stat_s, stat_r.at[j - 1], stat_sem, (j,), {"row": (r + j) % ROWS})

    def upg_copy(j, owner):
        return remote(upg.at[owner], upg.at[owner], upg_sem, (j,), {"depth": (d + j) % DEPTH})

    def dng_copy(j, owner):
        return remote(dng.at[owner], dng.at[owner], dng_sem, (j,), {"depth": (d + j) % DEPTH})

    for j in range(1, ROWS):
        stat_copy(j).start()

    def token_rows(k, col):
        return raw.at[k, pl.ds(pl.multiple_of(STEP * col, STEP), STEP)]

    def nlo_copy(k, col):
        return remote(token_rows(k, col), token_rows(k, col), nlo_sem, (k,), {"col": pc})

    def y_peer(j):
        return {"col": ((y + j) % YS) * 2 + lo}

    def nown_copy(k, j, col):
        return remote(token_rows(k, col), token_rows(k, col), nown_sem, (k, j), y_peer(j))

    def nfwd_copy(k, j, col):
        return remote(token_rows(k, col), token_rows(k, col), nfwd_sem, (k, j), y_peer(j))

    def ndiag_copy(j):
        peer = {"col": ((y + j) % YS) * 2 + (1 - lo)}
        return remote(token_rows(0, c), token_rows(0, c), nfwd_sem, (0, j), peer)

    for j in range(1, YS):
        ndiag_copy(j).start()
        nown_copy(0, j, c).start()

    nlo_copy(0, c).start()
    for j in range(1, DEPTH):
        dng_copy(j, d).start()
    for j in range(1, DEPTH):
        upg_copy(j, d).start()

    def forward_tokens(k):
        nlo_copy(k, pc).wait_recv()
        for j in range(1, YS):
            nfwd_copy(k, j, pc).start()

    gain_row[...] = gain[...].astype(f32).reshape(1, FEAT)
    shift_row[...] = shift[...].astype(f32).reshape(1, FEAT)
    bias_row[...] = bias[...].astype(f32).reshape(1, HID)
    for j in range(1, ROWS):
        stat_copy(j).wait_recv()
    total = stat_s[...] + stat_r[0] + stat_r[1] + stat_r[2]
    total = jnp.concatenate([total, jnp.zeros((120, 128), f32)], axis=0).T[0:OWN]
    count = 1.0 / (FEAT * ROWS)
    mean = total[:, 0:1] * count
    inv = lax.rsqrt(total[:, 1:2] * count - mean * mean + norm_epsilon)
    both = jnp.where(lane == 0, mean, inv)
    for k in range(CHUNKS):
        mst[k, pl.ds(pl.multiple_of(STEP * c, STEP), STEP), :] = both[STEP * k : STEP * (k + 1)]

    def mst_copy(late, j, col):
        rows = pl.ds(pl.multiple_of(STEP * col, STEP), STEP)
        ref = mst.at[pl.ds(1, CHUNKS - 1), rows] if late else mst.at[0, rows]
        return remote(ref, ref, mst_sem, (late, j), {"col": (c + j) % COLS})

    for late in (0, 1):
        for j in range(1, COLS):
            mst_copy(late, j, c).start()

    def send_own(k, carry):
        nlo_copy(k, c).start()
        for j in range(1, YS):
            nown_copy(k, j, c).start()
        return carry

    lax.fori_loop(1, CHUNKS, send_own, 0)

    def adapter_operands():
        for j in range(1, DEPTH):
            dng_copy(j, (d + DEPTH - j) % DEPTH).wait_recv()
        for i in range(DEPTH // 2):
            u = jnp.concatenate([dng[2 * i], dng[2 * i + 1]], axis=1)
            high = u.astype(bf16)
            mid_part = (u - high.astype(f32)).astype(bf16)
            zero = jnp.zeros_like(high)
            cols = slice(2 * DNB * i, 2 * DNB * (i + 1))
            d_low[:, cols] = jnp.concatenate([high, high, high, zero], axis=0)
            d_prod[:, cols] = jnp.concatenate([high, mid_part, high, zero], axis=0)
        for j in range(1, DEPTH):
            upg_copy(j, (d + DEPTH - j) % DEPTH).wait_recv()
        for i in range(DEPTH):
            u = upg[i]
            high = u.astype(bf16)
            mid_part = (u - high.astype(f32)).astype(bf16)
            zero = jnp.zeros_like(high)
            cols = slice(UPB * i, UPB * (i + 1))
            u_low[:, cols] = jnp.concatenate([high, high, high, zero], axis=0)
            u_prod[:, cols] = jnp.concatenate([high, mid_part, high, zero], axis=0)

    dn_acc[...] = jnp.zeros_like(dn_acc)
    w_copy.wait()
    cot_copy.wait()

    def split(value):
        high = value.astype(bf16).astype(f32)
        lanes = lax.broadcasted_iota(jnp.int32, value.shape, 1)
        return jnp.where(lanes < 2 * RANK, high, value - high).astype(bf16)

    def part_rows(k, owner, half):
        start = pl.multiple_of(RING * owner + STEP * half, STEP)
        return k, pl.ds(start, STEP)

    def rs_copy(k, slot):
        target = right if slot < 3 else left
        return remote(rs_s.at[k, slot], rs_r.at[k, slot], rs_sem, (k, slot), {"row": target})

    tail = lax.broadcasted_iota(jnp.int32, (STEP, 128), 1)

    def rs_decoder(k, slot):
        last = rs_r[k, slot, :, HID : HID + 128].astype(f32) * 1.0
        main = decoder(
            lambda t, n: last[:, 64:128] if t == HID else rs_r[k, slot, :, t : t + n], HID
        )
        scale = last[:, 96:97] * (1.0 / (CODE_SPAN * LN2))
        return main, jnp.where(tail < 2 * RANK, jnp.log(last) * scale, 0.0)

    def rs_send(k, slot, owner, half):
        kk, rows = part_rows(k, owner, half)
        value = part[kk, rows, HID : HID + 128]
        top = jnp.max(jnp.abs(value), axis=1, keepdims=True)
        top = (jnp.maximum(top, 1e-30) * 1.01).astype(bf16).astype(f32)
        code = jnp.exp2(value * (CODE_SPAN / top))

        def store(t, n, coded):
            if t == HID:
                scale = jnp.where(tail < 3 * RANK, coded.astype(f32), top)
                coded = jnp.where(tail < 2 * RANK, code, scale).astype(bf16)
            rs_s[k, slot, :, t : t + n] = coded

        encode(lambda t: part[kk, rows, t : t + TILE], store, STEP, HID)
        rs_copy(k, slot).start()

    def phase_forward(k):
        @pl.when(k == 0)
        def _():
            nlo_copy(0, pc).wait_recv()
            for j in range(1, COLS):
                mst_copy(0, j, (c + COLS - j) % COLS).wait_recv()

        @pl.when(k == 1)
        def _():
            for j in range(1, COLS):
                mst_copy(1, j, (c + COLS - j) % COLS).wait_recv()

        for j in range(1, YS):
            source = (y + YS - j) % YS
            nown_copy(k, j, source * 2 + lo).wait_recv()
            nfwd_copy(k, j, source * 2 + (1 - lo)).wait_recv()
        mean_, inv_ = mst[k, :, 0:1], mst[k, :, 1:2]
        for t in range(0, FEAT, TILE):
            cols = slice(t, t + TILE)
            nrm[k, :, cols] = (
                (raw[k, :, cols].astype(f32) - mean_) * inv_ * gain_row[:, cols]
                + shift_row[:, cols]
            ).astype(bf16)
        def rank_product():
            value = adapter_scale * lax.dot_general(
                nrm[k], d_low[...], NT, preferred_element_type=f32
            )
            part[k, :, HID : HID + 128] = value
            low[k] = split(value)

        def rank_tile(cols):
            return jnp.dot(low[k], u_prod[:, cols], preferred_element_type=f32)

        def columns(t):
            return pl.ds(pl.multiple_of(t * TILE, TILE), TILE)

        def main_tile(cols):
            return jnp.dot(nrm[k], w[:, cols], preferred_element_type=f32)

        @pl.when(k == 0)
        def _():
            def tile(t, carry):
                part[k, :, columns(t)] = main_tile(columns(t))
                return carry

            def add(t, carry):
                part[k, :, columns(t)] += rank_tile(columns(t))
                return carry

            lax.fori_loop(0, HID // TILE, tile, 0)
            adapter_operands()
            rank_product()
            lax.fori_loop(0, HID // TILE, add, 0)

        @pl.when(k > 0)
        def _():
            def tile(t, carry):
                part[k, :, columns(t)] = main_tile(columns(t)) + rank_tile(columns(t))
                return carry

            rank_product()
            lax.fori_loop(0, HID // TILE, tile, 0)

        rs_send(k, 0, opp, 0)
        rs_send(k, 3, opp, 1)
        rs_send(k, 1, right, 1)
        rs_send(k, 4, left, 0)

    def phase_relay(k):
        for slot, owner, half in ((0, right, 0), (3, left, 1)):
            rs_copy(k, slot).wait_recv()
            kk, rows = part_rows(k, owner, half)
            got, low_got = rs_decoder(k, slot)
            part[kk, rows, HID : HID + 128] += low_got
            for t in range(0, HID, TILE):
                part[kk, rows, t : t + TILE] += got(t)
            rs_send(k, slot + 2, owner, half)

    def slope_rows(k, owner, first, count_):
        return slg.at[k, pl.ds(pl.multiple_of(RING * owner + first, STEP), count_)]

    ag_half = (0, 1, 0, 1, 0, 1)

    def ag_copy(k, slot, owner):
        rows = slope_rows(k, owner, STEP * ag_half[slot], STEP)
        target = right if slot < 3 else left
        return remote(rows, rows, ag_sem, (k, slot), {"row": target})

    def phase_middle(k):
        for half, first, second in ((0, 4, 2), (1, 1, 5)):
            rs_copy(k, first).wait_recv()
            rs_copy(k, second).wait_recv()
            kk, rows = part_rows(k, r, half)
            (one, low_one), (two, low_two) = rs_decoder(k, first), rs_decoder(k, second)
            low_own[k, STEP * half : STEP * (half + 1), :] = (
                part[kk, rows, HID : HID + 128] + low_one + low_two
            )
            start = pl.multiple_of(OWN * half + STEP * k, STEP)
            for t in range(0, HID, TILE):
                cols = slice(t, t + TILE)
                v = part[kk, rows, cols] + one(t) + two(t) + bias_row[:, cols]
                value, slope = gelu_both(v)
                hidden[pl.ds(start, STEP), cols] = value.astype(bf16)
                slg[kk, rows, cols] = (
                    cot[pl.ds(start, STEP), cols].astype(f32) * slope
                ).astype(bf16)
            for slot in (0,) if half == 0 else (3, 1, 4):
                ag_copy(k, slot, r).start()

    def phase_spread(k):
        ag_copy(k, 0, left).wait_recv()
        ag_copy(k, 2, left).start()
        ag_copy(k, 3, right).wait_recv()
        ag_copy(k, 5, right).start()

    def cs_copy(k, j):
        return remote(cs_s.at[k, j - 1], cs_r.at[k, j - 1], cs_sem, (k, j), y_peer(j))

    def ug_copy(j):
        peer = (d + j) % DEPTH
        return remote(ugs.at[peer], ugr.at[j], ug_sem, (j,), {"depth": peer})

    def dg_copy(j):
        peer = (d + j) % DEPTH
        return remote(dgs.at[peer], dgr.at[j], dg_sem, (j,), {"depth": peer})

    def ux_copy(j, owner):
        return remote(upx.at[owner], upx.at[owner], ux_sem, (j,), {"row": (r + j) % ROWS})

    def dx_copy(j, owner):
        return remote(dnx.at[owner], dnx.at[owner], dx_sem, (j,), {"col": (c + j) % COLS})

    def down_send():
        for i in range(DEPTH):
            dgs[i] = dn_acc[:, DNB * i : DNB * (i + 1)]
        for j in range(1, DEPTH):
            dg_copy(j).start()

    def up_send():
        lanes = lax.broadcasted_iota(jnp.int32, (RING, 128), 1)
        sides = []
        for k in range(CHUNKS):
            value = low_own[k]
            high = value.astype(bf16).astype(f32)
            both_parts = jnp.where(
                lanes < RANK, high, jnp.where(lanes < 2 * RANK, value - high, 0.0)
            )
            sides.append(both_parts.T.astype(bf16))
        for i in range(DEPTH):
            cols = slice(UPB * i, UPB * (i + 1))
            g = jnp.zeros((128, UPB), f32)
            for k in range(CHUNKS):
                rows = pl.ds(pl.multiple_of(RING * r, RING), RING)
                g += jnp.dot(sides[k], slg[k, rows, cols], preferred_element_type=f32)
            ugs[i] = g[0:RANK] + g[RANK : 2 * RANK]
        for j in range(1, DEPTH):
            ug_copy(j).start()

    def phase_backward(k):
        ag_copy(k, 1, left).wait_recv()
        ag_copy(k, 4, right).wait_recv()
        ag_copy(k, 2, opp).wait_recv()
        ag_copy(k, 5, opp).wait_recv()
        slopes = slg[k]
        rank = split(
            adapter_scale * lax.dot_general(slopes, u_low[...], NT, preferred_element_type=f32)
        )
        rank_t = rank.astype(f32).T.astype(bf16)

        def grow_down(t, carry):
            cols = pl.ds(pl.multiple_of(t * TILE, TILE), TILE)
            g = jnp.dot(rank_t, nrm[k, :, cols], preferred_element_type=f32)
            dn_acc[:, cols] += g[0:RANK] + g[2 * RANK : 3 * RANK]
            return carry

        lax.fori_loop(0, FEAT // TILE, grow_down, 0)

        @pl.when(k == CHUNKS - 1)
        def _():
            down_send()

        bsize = 256

        def tile(t, carry):
            rows = pl.ds(pl.multiple_of(t * bsize, bsize), bsize)
            back[k, :, rows] = lax.dot_general(
                slg[k], w[rows, :], NT, preferred_element_type=f32
            ) + jnp.dot(rank, d_prod[:, rows], preferred_element_type=f32)
            return carry

        lax.fori_loop(0, FEAT // bsize, tile, 0)
        for j in range(1, YS):
            rows = pl.ds(pl.multiple_of(RING * ((y + j) % YS), RING), RING)

            def store(t, n, value):
                cs_s[k, j - 1, :, t : t + n] = value

            encode(lambda t: back[k, rows, t : t + TILE], store, RING, FEAT)
            cs_copy(k, j).start()

    def lo_copy(k):
        return remote(lo_s.at[k], lo_r.at[k], lo_sem, (k,), {"col": pc})

    def phase_fold(k):
        mine = pl.ds(pl.multiple_of(RING * y, RING), RING)
        for j in range(1, YS):
            cs_copy(k, j).wait_recv()
            got = decoder(lambda t, n: cs_r[k, j - 1, :, t : t + n], FEAT)
            for t in range(0, FEAT, TILE):
                back[k, mine, t : t + TILE] += got(t)
        other = pl.ds(pl.multiple_of(RING * y + STEP * (1 - lo), STEP), STEP)

        def store(t, n, value):
            lo_s[k, :, t : t + n] = value

        encode(lambda t: back[k, other, t : t + TILE], store, STEP, FEAT)
        lo_copy(k).start()

    def gst_copy(k, j):
        return remote(gst_s.at[k], gst_r.at[k, j - 1], gst_sem, (k, j), {"row": (r + j) % ROWS})

    def own_rows(k):
        return pl.ds(pl.multiple_of(STEP * k, STEP), STEP)

    def own_centred(k, cols):
        rows = pl.ds(pl.multiple_of(STEP * c, STEP), STEP)
        return (tok[own_rows(k), cols].astype(f32) - mst[k, rows, 0:1]) * mst[k, rows, 1:2]

    def phase_stats(k):
        lo_copy(k).wait_recv()
        mine = pl.ds(pl.multiple_of(RING * y + STEP * lo, STEP), STEP)
        got = decoder(lambda t, n: lo_r[k, :, t : t + n], FEAT)
        one = jnp.zeros((STEP, 1), f32)
        two = jnp.zeros((STEP, 1), f32)
        for t in range(0, FEAT, TILE):
            cols = slice(t, t + TILE)
            scaled = (back[k, mine, cols] + got(t)) * gain_row[:, cols]
            ng[k, :, cols] = scaled
            one += jnp.sum(scaled, axis=1, keepdims=True)
            two += jnp.sum(scaled * own_centred(k, cols), axis=1, keepdims=True)
        lanes = lax.broadcasted_iota(jnp.int32, (STEP, 128), 1)
        gst_s[k] = jnp.where(lanes == 0, one, jnp.where(lanes == 1, two, 0.0))
        for j in range(1, ROWS):
            gst_copy(k, j).start()

    def phase_finish(k):
        for j in range(1, ROWS):
            gst_copy(k, j).wait_recv()
        sums = (gst_s[k] + gst_r[k, 0] + gst_r[k, 1] + gst_r[k, 2]) * count
        inv_ = mst[k, pl.ds(pl.multiple_of(STEP * c, STEP), STEP), 1:2]
        for t in range(0, FEAT, TILE):
            cols = slice(t, t + TILE)
            input_grad[own_rows(k), cols] = (
                inv_ * (ng[k, :, cols] - sums[:, 0:1] - own_centred(k, cols) * sums[:, 1:2])
            ).astype(bf16)

    def grads_spread():
        up_sum = ugs[d]
        dn_sum = dgs[d]
        for j in range(1, DEPTH):
            ug_copy(j).wait_recv()
            dg_copy(j).wait_recv()
            up_sum += ugr[j]
            dn_sum += dgr[j]
        upx[r] = up_sum
        dnx[c] = dn_sum
        for j in range(1, ROWS):
            ux_copy(j, r).start()
        for j in range(1, COLS):
            dx_copy(j, c).start()

    def drain_early():
        for j in range(1, ROWS):
            stat_copy(j).wait_send()
        for j in range(1, COLS):
            mst_copy(0, j, c).wait_send()
            mst_copy(1, j, c).wait_send()
        for j in range(1, DEPTH):
            dng_copy(j, d).wait_send()
            upg_copy(j, d).wait_send()
        for j in range(1, YS):
            ndiag_copy(j).wait_send()

        def drain_tokens(k, carry):
            for j in range(1, YS):
                nfwd_copy(k, j, pc).wait_send()
            return carry

        def drain(k, carry):
            nlo_copy(k, c).wait_send()
            for j in range(1, YS):
                nown_copy(k, j, c).wait_send()
            for slot in range(6):
                rs_copy(k, slot).wait_send()
            return carry

        lax.fori_loop(0, CHUNKS, drain, 0)
        lax.fori_loop(1, CHUNKS, drain_tokens, 0)

    def iteration(it, carry):
        def step(condition, run):
            pl.when(condition)(run)

        step(it < CHUNKS, lambda: phase_forward(it))

        @pl.when(it == 0)
        def _():
            for k in range(1, CHUNKS):
                forward_tokens(k)

        step((it >= 2) & (it < CHUNKS), lambda: phase_spread(it - 2))
        step(it < CHUNKS, lambda: phase_relay(it))
        step((it >= 1) & (it < CHUNKS + 1), lambda: phase_middle(it - 1))
        step((it >= CHUNKS) & (it < CHUNKS + 2), lambda: phase_spread(it - 2))
        step(it == CHUNKS, up_send)
        step(it == CHUNKS + 2, drain_early)
        step((it >= 3) & (it < CHUNKS + 3), lambda: phase_backward(it - 3))
        step(it == CHUNKS + 2, grads_spread)
        step(it >= CHUNKS + 2, lambda: phase_finish(it - CHUNKS - 2))
        step((it >= CHUNKS + 1) & (it < CHUNKS * 2 + 1), lambda: phase_stats(it - CHUNKS - 1))
        step((it >= CHUNKS) & (it < CHUNKS * 2), lambda: phase_fold(it - CHUNKS))
        return carry

    lax.fori_loop(0, CHUNKS * 2 + 2, iteration, 0)

    for j in range(1, ROWS):
        ux_copy(j, (r + ROWS - j) % ROWS).wait_recv()
    for j in range(1, COLS):
        dx_copy(j, (c + COLS - j) % COLS).wait_recv()
    up_gradient = upx[0]
    for i in range(1, ROWS):
        up_gradient += upx[i]
    down_gradient = dnx[0]
    for i in range(1, COLS):
        down_gradient += dnx[i]
    up_grad[...] = up_gradient
    down_grad[...] = down_gradient

    for j in range(1, ROWS):
        ux_copy(j, r).wait_send()
    for j in range(1, COLS):
        dx_copy(j, c).wait_send()
    for j in range(1, DEPTH):
        ug_copy(j).wait_send()
        dg_copy(j).wait_send()

    def drain(k, carry):
        for j in range(1, YS):
            cs_copy(k, j).wait_send()
        for slot, owner in ((0, r), (1, r), (2, left), (3, r), (4, r), (5, right)):
            ag_copy(k, slot, owner).wait_send()
        lo_copy(k).wait_send()
        for j in range(1, ROWS):
            gst_copy(k, j).wait_send()
        return carry

    lax.fori_loop(0, CHUNKS, drain, 0)


def update_kernel(
    hidden,
    input_grad,
    down_grad,
    up_grad,
    down_w,
    up_w,
    down_m,
    down_s,
    up_m,
    up_s,
    hidden_out,
    input_grad_out,
    new_down_w,
    new_down_m,
    new_down_s,
    new_up_w,
    new_up_m,
    new_up_s,
    sems,
):
    copies = (
        pltpu.make_async_copy(hidden, hidden_out, sems.at[0]),
        pltpu.make_async_copy(input_grad, input_grad_out, sems.at[1]),
    )
    for copy in copies:
        copy.start()
    new_up_w[...], new_up_m[...], new_up_s[...] = adam(
        up_w[...], up_m[...], up_s[...], up_grad[...]
    )
    new_down_w[...], new_down_m[...], new_down_s[...] = adam(
        down_w[...], down_m[...], down_s[...], down_grad[...]
    )
    for copy in copies:
        copy.wait()


def shards(*blocks):
    (tok, w, bias, gain, shift, down_w, up_w, down_m, down_s, up_m, up_s, cot) = blocks
    vmem = pl.BlockSpec(memory_space=pltpu.VMEM)
    hbm = pl.BlockSpec(memory_space=pl.ANY)
    n = CHUNKS
    dma = pltpu.SemaphoreType.DMA
    small = jax.ShapeDtypeStruct((RANK, DNB), f32)
    wide = jax.ShapeDtypeStruct((RANK, UPB), f32)
    scratch = [
        pltpu.VMEM((FEAT, HID), bf16),
        pltpu.VMEM((2 * OWN, HID), bf16),
        dma((2,)),
        pltpu.VMEM((8, 128), f32),
        pltpu.VMEM((ROWS - 1, 8, 128), f32),
        pltpu.VMEM((1, FEAT), f32),
        pltpu.VMEM((1, FEAT), f32),
        pltpu.VMEM((1, HID), f32),
        pltpu.VMEM((n, TOK, FEAT), bf16),
        pltpu.VMEM((n, TOK, 128), f32),
        pltpu.VMEM((n, TOK, FEAT), bf16),
        pltpu.VMEM((DEPTH, RANK, UPB), f32),
        pltpu.VMEM((DEPTH, RANK, DNB), f32),
        pltpu.VMEM((4 * RANK, FEAT), bf16),
        pltpu.VMEM((4 * RANK, FEAT), bf16),
        pltpu.VMEM((4 * RANK, HID), bf16),
        pltpu.VMEM((4 * RANK, HID), bf16),
        pltpu.VMEM((n, TOK, HID + 128), f32),
        pltpu.VMEM((n, TOK, 4 * RANK), bf16),
        pltpu.VMEM((n, 6, STEP, HID + 128), bf16),
        pltpu.VMEM((n, 6, STEP, HID + 128), bf16),
        pltpu.VMEM((n, TOK, HID), bf16),
        pltpu.VMEM((n, TOK, FEAT), f32),
        pltpu.VMEM((n, YS - 1, RING, FEAT + 128), bf16),
        pltpu.VMEM((n, YS - 1, RING, FEAT + 128), bf16),
        pltpu.VMEM((n, STEP, FEAT + 128), bf16),
        pltpu.VMEM((n, STEP, FEAT + 128), bf16),
        pltpu.VMEM((n, STEP, FEAT), f32),
        pltpu.VMEM((n, STEP, 128), f32),
        pltpu.VMEM((n, ROWS - 1, STEP, 128), f32),
        pltpu.VMEM((n, RING, 128), f32),
        pltpu.VMEM((RANK, FEAT), f32),
        pltpu.VMEM((DEPTH, RANK, UPB), f32),
        pltpu.VMEM((DEPTH, RANK, UPB), f32),
        pltpu.VMEM((DEPTH, RANK, DNB), f32),
        pltpu.VMEM((DEPTH, RANK, DNB), f32),
        pltpu.VMEM((ROWS, RANK, UPB), f32),
        pltpu.VMEM((COLS, RANK, DNB), f32),
        dma((2, ROWS)),
        dma((2, 2, COLS)),
        dma((2, n)),
        dma((2, n, YS)),
        dma((2, n, YS)),
        dma((2, DEPTH)),
        dma((2, DEPTH)),
        dma((2, n, 6)),
        dma((2, n, 6)),
        dma((2, n, YS)),
        dma((2, n)),
        dma((2, n, ROWS)),
        dma((2, DEPTH)),
        dma((2, DEPTH)),
        dma((2, ROWS)),
        dma((2, COLS)),
    ]
    outs = pl.pallas_call(
        kernel,
        out_shape=(
            jax.ShapeDtypeStruct((2 * OWN, HID), bf16),
            jax.ShapeDtypeStruct((OWN, FEAT), bf16),
            small,
            wide,
        ),
        in_specs=[vmem, hbm] + [vmem] * 5 + [hbm],
        out_specs=(vmem,) * 4,
        scratch_shapes=scratch,
        compiler_params=pltpu.CompilerParams(
            collective_id=0, has_side_effects=True, vmem_limit_bytes=56 * 1024 * 1024
        ),
        cost_estimate=pl.CostEstimate(
            flops=4 * 512 * FEAT * HID, bytes_accessed=14000000, transcendentals=10000000
        ),
        name="fused_step",
    )(tok, w, bias, gain, shift, down_w, up_w, cot)
    return pl.pallas_call(
        update_kernel,
        out_shape=(
            jax.ShapeDtypeStruct((2 * OWN, HID), bf16),
            jax.ShapeDtypeStruct((OWN, FEAT), bf16),
            small,
            small,
            small,
            wide,
            wide,
            wide,
        ),
        in_specs=[vmem] * 10,
        out_specs=(hbm, hbm) + (vmem,) * 6,
        scratch_shapes=[dma((2,))],
        name="adapter_update",
    )(*outs, down_w, up_w, down_m, down_s, up_m, up_s)


def solution(mesh):
    down = P(None, ("row", "depth"))
    up = P(None, ("col", "depth"))
    return jax.shard_map(
        shards,
        mesh=mesh,
        in_specs=(
            P(("depth", "col"), "row"),
            P("row", "col"),
            P("col"),
            P("row"),
            P("row"),
            down,
            up,
            down,
            down,
            up,
            up,
            P(("depth", "row"), "col"),
        ),
        out_specs=(
            P(("depth", "row"), "col"),
            P(("depth", "col"), "row"),
            down,
            down,
            down,
            up,
            up,
            up,
        ),
        check_vma=False,
    )
```

```python
import functools
import jax
import jax.numpy as jnp
from jax import lax
from jax.experimental import pallas as pl
from jax.experimental.pallas import tpu as pltpu
from jax.sharding import PartitionSpec as P

adapter_scale = 0.5
norm_epsilon = 1e-05
beta_first = 0.9
beta_second = 0.999
adam_step = 10
learn_rate = 0.01
decay_rate = 0.1
adam_epsilon = 1e-08

f32 = jnp.float32
bf16 = jnp.bfloat16
MESH = pl.DeviceIdType.MESH
NT = (((1,), (1,)), ((), ()))

ROWS, COLS, DEPTH = 4, 8, 8
YS = COLS // 2
CHUNKS = 4
OWN = 64
STEP = OWN // CHUNKS
TOK = STEP * COLS
FEAT, HID, RANK = 1536, 3072, 32
UPB, DNB = HID // DEPTH, FEAT // DEPTH
RING = 2 * STEP
CODE_SPAN = 120.0
LN2 = 0.6931471805599453
TILE = 512
WIDE = 1024
LAST = CHUNKS - 1


def gelu_both(v):
    inner = 0.7978845608 * (v + 0.044715 * v * v * v)
    tangent = jnp.tanh(inner)
    value = 0.5 * v * (1.0 + tangent)
    slope = 0.5 * (1.0 + tangent) + 0.5 * v * (1.0 - tangent * tangent) * 0.7978845608 * (
        1.0 + 3.0 * 0.044715 * v * v
    )
    return value, slope


def adam(weight, moment, square, gradient):
    new_moment = beta_first * moment + (1.0 - beta_first) * gradient
    new_square = beta_second * square + (1.0 - beta_second) * gradient * gradient
    update = (
        new_moment
        / (1.0 - beta_first**adam_step)
        / (jnp.sqrt(new_square / (1.0 - beta_second**adam_step)) + adam_epsilon)
    )
    return weight - learn_rate * (update + decay_rate * weight), new_moment, new_square


def encode(load, store, rows, width):
    top = jnp.zeros((rows, 1), f32)
    for t in range(0, width, TILE):
        top = jnp.maximum(top, jnp.max(jnp.abs(load(t)), axis=1, keepdims=True))
    top = (jnp.maximum(top, 1e-30) * 1.01).astype(bf16)
    factor = CODE_SPAN / top.astype(f32)
    for t in range(0, width, TILE):
        store(t, TILE, jnp.exp2(load(t) * factor).astype(bf16))
    store(width, 128, jnp.broadcast_to(top, (rows, 128)))


def decoder(load, width):
    scale = load(width, 128)[:, 0:1].astype(f32) * (1.0 / (CODE_SPAN * LN2))
    return lambda t: jnp.log(load(t, TILE).astype(f32)) * scale


def kernel(
    tok,
    w_hbm,
    bias,
    gain,
    shift,
    down_w,
    up_w,
    cot_hbm,
    hidden,
    input_grad,
    down_grad,
    up_grad,
    w,
    cot,
    local_sem,
    stat_s,
    stat_r,
    gain_row,
    shift_row,
    bias_row,
    raw,
    mst,
    nrm,
    upg,
    dng,
    d_low,
    d_prod,
    u_low,
    u_prod,
    part,
    low,
    rs_s,
    rs_r,
    slg,
    back,
    cs_s,
    cs_r,
    lo_s,
    lo_r,
    ng,
    gst_s,
    gst_r,
    xs_s,
    xs_r,
    sst_s,
    sst_r,
    sct_s,
    sct_r,
    stt,
    low_own,
    dn_acc,
    ugs,
    ugr,
    dgs,
    dgr,
    upx,
    dnx,
    stat_sem,
    mst_sem,
    nlo_sem,
    nown_sem,
    nfwd_sem,
    upg_sem,
    dng_sem,
    rs_sem,
    ag_sem,
    cs_sem,
    lo_sem,
    gst_sem,
    xs_sem,
    sst_sem,
    sct_sem,
    ug_sem,
    dg_sem,
    ux_sem,
    dx_sem,
):
    r = lax.axis_index("row")
    c = lax.axis_index("col")
    d = lax.axis_index("depth")
    y, lo = c // 2, c % 2
    right, left, opp = (r + 1) % ROWS, (r + 3) % ROWS, (r + 2) % ROWS
    pc = y * 2 + (1 - lo)

    def remote(src, dst, sems, index, device):
        return pltpu.make_async_remote_copy(
            src_ref=src,
            dst_ref=dst,
            send_sem=sems.at[(0,) + index],
            recv_sem=sems.at[(1,) + index],
            device_id=device,
            device_id_type=MESH,
        )

    w_copy = pltpu.make_async_copy(w_hbm, w, local_sem.at[0])
    cot_copy = pltpu.make_async_copy(cot_hbm, cot, local_sem.at[1])
    w_copy.start()
    cot_copy.start()

    barrier = pltpu.get_barrier_semaphore()
    for j in range(1, ROWS):
        pl.semaphore_signal(barrier, inc=1, device_id={"row": (r + j) % ROWS}, device_id_type=MESH)
    for j in range(1, COLS):
        pl.semaphore_signal(barrier, inc=1, device_id={"col": (c + j) % COLS}, device_id_type=MESH)
    for j in range(1, DEPTH):
        pl.semaphore_signal(
            barrier, inc=1, device_id={"depth": (d + j) % DEPTH}, device_id_type=MESH
        )

    x = tok[...].astype(f32)
    lane = lax.broadcasted_iota(jnp.int32, (OWN, 128), 1)
    s1 = jnp.sum(x, axis=1, keepdims=True)
    s2 = jnp.sum(x * x, axis=1, keepdims=True)
    sums = jnp.where(lane == 0, s1, jnp.where(lane == 1, s2, 0.0))
    stat_s[...] = jnp.concatenate([sums, jnp.zeros_like(sums)], axis=0).T[0:8]
    upg[d] = up_w[...]
    dng[d] = down_w[...]
    for k in range(CHUNKS):
        raw[k, pl.ds(pl.multiple_of(STEP * c, STEP), STEP), :] = tok[STEP * k : STEP * (k + 1), :]
    pl.semaphore_wait(barrier, ROWS + COLS + DEPTH - 3)

    def stat_copy(j):
        return remote(stat_s, stat_r.at[j - 1], stat_sem, (j,), {"row": (r + j) % ROWS})

    def upg_copy(j, owner):
        return remote(upg.at[owner], upg.at[owner], upg_sem, (j,), {"depth": (d + j) % DEPTH})

    def dng_copy(j, owner):
        return remote(dng.at[owner], dng.at[owner], dng_sem, (j,), {"depth": (d + j) % DEPTH})

    for j in range(1, ROWS):
        stat_copy(j).start()

    def token_rows(k, col):
        return raw.at[k, pl.ds(pl.multiple_of(STEP * col, STEP), STEP)]

    def nlo_copy(k, col):
        return remote(token_rows(k, col), token_rows(k, col), nlo_sem, (k,), {"col": pc})

    def y_peer(j):
        return {"col": ((y + j) % YS) * 2 + lo}

    def nown_copy(k, j, col):
        return remote(token_rows(k, col), token_rows(k, col), nown_sem, (k, j), y_peer(j))

    def nfwd_copy(k, j, col):
        return remote(token_rows(k, col), token_rows(k, col), nfwd_sem, (k, j), y_peer(j))

    def ndiag_copy(j):
        peer = {"col": ((y + j) % YS) * 2 + (1 - lo)}
        return remote(token_rows(0, c), token_rows(0, c), nfwd_sem, (0, j), peer)

    for j in range(1, YS):
        ndiag_copy(j).start()
        nown_copy(0, j, c).start()

    nlo_copy(0, c).start()
    for j in range(1, DEPTH):
        dng_copy(j, d).start()
    for j in range(1, DEPTH):
        upg_copy(j, d).start()

    def forward_tokens(k):
        nlo_copy(k, pc).wait_recv()
        for j in range(1, YS):
            nfwd_copy(k, j, pc).start()

    gain_row[...] = gain[...].astype(f32).reshape(1, FEAT)
    shift_row[...] = shift[...].astype(f32).reshape(1, FEAT)
    bias_row[...] = bias[...].astype(f32).reshape(1, HID)
    for j in range(1, ROWS):
        stat_copy(j).wait_recv()
    total = stat_s[...] + stat_r[0] + stat_r[1] + stat_r[2]
    total = jnp.concatenate([total, jnp.zeros((120, 128), f32)], axis=0).T[0:OWN]
    count = 1.0 / (FEAT * ROWS)
    mean = total[:, 0:1] * count
    inv = lax.rsqrt(total[:, 1:2] * count - mean * mean + norm_epsilon)
    both = jnp.where(lane == 0, mean, inv)
    for k in range(CHUNKS):
        mst[k, pl.ds(pl.multiple_of(STEP * c, STEP), STEP), :] = both[STEP * k : STEP * (k + 1)]

    def mst_copy(late, j, col):
        rows = pl.ds(pl.multiple_of(STEP * col, STEP), STEP)
        ref = mst.at[pl.ds(1, CHUNKS - 1), rows] if late else mst.at[0, rows]
        return remote(ref, ref, mst_sem, (late, j), {"col": (c + j) % COLS})

    for late in (0, 1):
        for j in range(1, COLS):
            mst_copy(late, j, c).start()

    def send_own(k, carry):
        nlo_copy(k, c).start()
        for j in range(1, YS):
            nown_copy(k, j, c).start()
        return carry

    lax.fori_loop(1, CHUNKS, send_own, 0)

    def adapter_operands():
        for j in range(1, DEPTH):
            dng_copy(j, (d + DEPTH - j) % DEPTH).wait_recv()
        for i in range(DEPTH // 2):
            u = jnp.concatenate([dng[2 * i], dng[2 * i + 1]], axis=1)
            high = u.astype(bf16)
            mid_part = (u - high.astype(f32)).astype(bf16)
            zero = jnp.zeros_like(high)
            cols = slice(2 * DNB * i, 2 * DNB * (i + 1))
            d_low[:, cols] = jnp.concatenate([high, high, high, zero], axis=0)
            d_prod[:, cols] = jnp.concatenate([high, mid_part, high, zero], axis=0)
        for j in range(1, DEPTH):
            upg_copy(j, (d + DEPTH - j) % DEPTH).wait_recv()
        for i in range(DEPTH):
            u = upg[i]
            high = u.astype(bf16)
            mid_part = (u - high.astype(f32)).astype(bf16)
            zero = jnp.zeros_like(high)
            cols = slice(UPB * i, UPB * (i + 1))
            u_low[:, cols] = jnp.concatenate([high, high, high, zero], axis=0)
            u_prod[:, cols] = jnp.concatenate([high, mid_part, high, zero], axis=0)

    dn_acc[...] = jnp.zeros_like(dn_acc)
    w_copy.wait()
    cot_copy.wait()

    def split(value):
        high = value.astype(bf16).astype(f32)
        lanes = lax.broadcasted_iota(jnp.int32, value.shape, 1)
        return jnp.where(lanes < 2 * RANK, high, value - high).astype(bf16)

    def part_rows(k, owner, half):
        start = pl.multiple_of(RING * owner + STEP * half, STEP)
        return k, pl.ds(start, STEP)

    def rs_copy(k, slot):
        target = right if slot < 3 else left
        return remote(rs_s.at[k, slot], rs_r.at[k, slot], rs_sem, (k, slot), {"row": target})

    tail = lax.broadcasted_iota(jnp.int32, (STEP, 128), 1)

    def rs_decoder(k, slot):
        last = rs_r[k, slot, :, HID : HID + 128].astype(f32) * 1.0
        main = decoder(
            lambda t, n: last[:, 64:128] if t == HID else rs_r[k, slot, :, t : t + n], HID
        )
        scale = last[:, 96:97] * (1.0 / (CODE_SPAN * LN2))
        return main, jnp.where(tail < 2 * RANK, jnp.log(last) * scale, 0.0)

    def rs_send(k, slot, owner, half):
        kk, rows = part_rows(k, owner, half)
        value = part[kk, rows, HID : HID + 128]
        top = jnp.max(jnp.abs(value), axis=1, keepdims=True)
        top = (jnp.maximum(top, 1e-30) * 1.01).astype(bf16).astype(f32)
        code = jnp.exp2(value * (CODE_SPAN / top))

        def store(t, n, coded):
            if t == HID:
                scale = jnp.where(tail < 3 * RANK, coded.astype(f32), top)
                coded = jnp.where(tail < 2 * RANK, code, scale).astype(bf16)
            rs_s[k, slot, :, t : t + n] = coded

        encode(lambda t: part[kk, rows, t : t + TILE], store, STEP, HID)
        rs_copy(k, slot).start()

    def phase_forward(k):
        @pl.when(k == 0)
        def _():
            nlo_copy(0, pc).wait_recv()
            for j in range(1, COLS):
                mst_copy(0, j, (c + COLS - j) % COLS).wait_recv()

        @pl.when(k == 1)
        def _():
            for j in range(1, COLS):
                mst_copy(1, j, (c + COLS - j) % COLS).wait_recv()

        for j in range(1, YS):
            source = (y + YS - j) % YS
            nown_copy(k, j, source * 2 + lo).wait_recv()
            nfwd_copy(k, j, source * 2 + (1 - lo)).wait_recv()
        mean_, inv_ = mst[k, :, 0:1], mst[k, :, 1:2]
        for t in range(0, FEAT, TILE):
            cols = slice(t, t + TILE)
            nrm[k, :, cols] = (
                (raw[k, :, cols].astype(f32) - mean_) * inv_ * gain_row[:, cols]
                + shift_row[:, cols]
            ).astype(bf16)
        def rank_product():
            value = adapter_scale * lax.dot_general(
                nrm[k], d_low[...], NT, preferred_element_type=f32
            )
            part[k, :, HID : HID + 128] = value
            low[k] = split(value)

        def rank_tile(cols):
            return jnp.dot(low[k], u_prod[:, cols], preferred_element_type=f32)

        def columns(t):
            return pl.ds(pl.multiple_of(t * WIDE, WIDE), WIDE)

        def main_tile(cols):
            return jnp.dot(nrm[k], w[:, cols], preferred_element_type=f32)

        @pl.when(k == 0)
        def _():
            def tile(t, carry):
                part[k, :, columns(t)] = main_tile(columns(t))
                return carry

            def add(t, carry):
                part[k, :, columns(t)] += rank_tile(columns(t))
                return carry

            lax.fori_loop(0, HID // WIDE, tile, 0)
            adapter_operands()
            rank_product()
            lax.fori_loop(0, HID // WIDE, add, 0)

        @pl.when(k > 0)
        def _():
            def tile(t, carry):
                part[k, :, columns(t)] = main_tile(columns(t)) + rank_tile(columns(t))
                return carry

            rank_product()
            lax.fori_loop(0, HID // WIDE, tile, 0)

        rs_send(k, 0, opp, 0)
        rs_send(k, 3, opp, 1)
        rs_send(k, 1, right, 1)
        rs_send(k, 4, left, 0)

    def phase_relay(k):
        for slot, owner, half in ((0, right, 0), (3, left, 1)):
            rs_copy(k, slot).wait_recv()
            kk, rows = part_rows(k, owner, half)
            got, low_got = rs_decoder(k, slot)
            part[kk, rows, HID : HID + 128] += low_got
            for t in range(0, HID, TILE):
                part[kk, rows, t : t + TILE] += got(t)
            rs_send(k, slot + 2, owner, half)

    def slope_rows(k, owner, first, count_):
        return slg.at[k, pl.ds(pl.multiple_of(RING * owner + first, STEP), count_)]

    ag_half = (0, 1, 0, 1, 0, 1)

    def ag_copy(k, slot, owner):
        rows = slope_rows(k, owner, STEP * ag_half[slot], STEP)
        target = right if slot < 3 else left
        return remote(rows, rows, ag_sem, (k, slot), {"row": target})

    def phase_middle(k):
        for half, first, second in ((0, 4, 2), (1, 1, 5)):
            rs_copy(k, first).wait_recv()
            rs_copy(k, second).wait_recv()
            kk, rows = part_rows(k, r, half)
            (one, low_one), (two, low_two) = rs_decoder(k, first), rs_decoder(k, second)
            low_own[k, STEP * half : STEP * (half + 1), :] = (
                part[kk, rows, HID : HID + 128] + low_one + low_two
            )
            start = pl.multiple_of(OWN * half + STEP * k, STEP)
            for t in range(0, HID, TILE):
                cols = slice(t, t + TILE)
                v = part[kk, rows, cols] + one(t) + two(t) + bias_row[:, cols]
                value, slope = gelu_both(v)
                hidden[pl.ds(start, STEP), cols] = value.astype(bf16)
                slg[kk, rows, cols] = (
                    cot[pl.ds(start, STEP), cols].astype(f32) * slope
                ).astype(bf16)
            for slot in (0,) if half == 0 else (3, 1, 4):
                ag_copy(k, slot, r).start()

    def phase_spread(k):
        ag_copy(k, 0, left).wait_recv()
        ag_copy(k, 2, left).start()
        ag_copy(k, 3, right).wait_recv()
        ag_copy(k, 5, right).start()

    def cs_copy(k, j):
        return remote(cs_s.at[k, j - 1], cs_r.at[k, j - 1], cs_sem, (k, j), y_peer(j))

    def ug_copy(j):
        peer = (d + j) % DEPTH
        return remote(ugs.at[peer], ugr.at[j], ug_sem, (j,), {"depth": peer})

    def dg_copy(j):
        peer = (d + j) % DEPTH
        return remote(dgs.at[peer], dgr.at[j], dg_sem, (j,), {"depth": peer})

    def ux_copy(j, owner):
        return remote(upx.at[owner], upx.at[owner], ux_sem, (j,), {"row": (r + j) % ROWS})

    def dx_copy(j, owner):
        return remote(dnx.at[owner], dnx.at[owner], dx_sem, (j,), {"col": (c + j) % COLS})

    def down_send():
        for i in range(DEPTH):
            dgs[i] = dn_acc[:, DNB * i : DNB * (i + 1)]
        for j in range(1, DEPTH):
            dg_copy(j).start()

    def up_send():
        lanes = lax.broadcasted_iota(jnp.int32, (RING, 128), 1)
        sides = []
        for k in range(CHUNKS):
            value = low_own[k]
            high = value.astype(bf16).astype(f32)
            both_parts = jnp.where(
                lanes < RANK, high, jnp.where(lanes < 2 * RANK, value - high, 0.0)
            )
            sides.append(both_parts.T.astype(bf16))
        for i in range(DEPTH):
            cols = slice(UPB * i, UPB * (i + 1))
            g = jnp.zeros((128, UPB), f32)
            for k in range(CHUNKS):
                rows = pl.ds(pl.multiple_of(RING * r, RING), RING)
                g += jnp.dot(sides[k], slg[k, rows, cols], preferred_element_type=f32)
            ugs[i] = g[0:RANK] + g[RANK : 2 * RANK]
        for j in range(1, DEPTH):
            ug_copy(j).start()

    def phase_backward(k):
        ag_copy(k, 1, left).wait_recv()
        ag_copy(k, 4, right).wait_recv()
        ag_copy(k, 2, opp).wait_recv()
        ag_copy(k, 5, opp).wait_recv()
        slopes = slg[k]
        rank = split(
            adapter_scale * lax.dot_general(slopes, u_low[...], NT, preferred_element_type=f32)
        )
        rank_t = rank.astype(f32).T.astype(bf16)

        def grow_down(t, carry):
            cols = pl.ds(pl.multiple_of(t * TILE, TILE), TILE)
            g = jnp.dot(rank_t, nrm[k, :, cols], preferred_element_type=f32)
            dn_acc[:, cols] += g[0:RANK] + g[2 * RANK : 3 * RANK]
            return carry

        lax.fori_loop(0, FEAT // TILE, grow_down, 0)

        @pl.when(k == CHUNKS - 1)
        def _():
            down_send()

        bsize = 768

        def tile(t, carry):
            rows = pl.ds(pl.multiple_of(t * bsize, bsize), bsize)
            back[k, :, rows] = lax.dot_general(
                slg[k], w[rows, :], NT, preferred_element_type=f32
            ) + jnp.dot(rank, d_prod[:, rows], preferred_element_type=f32)
            return carry

        lax.fori_loop(0, FEAT // bsize, tile, 0)
        pl.when(k < LAST)(lambda: fold_send(k))
        pl.when(k == LAST)(last_send)

    def fold_send(k):
        for j in range(1, YS):
            rows = pl.ds(pl.multiple_of(RING * ((y + j) % YS), RING), RING)

            def store(t, n, value):
                cs_s[k, j - 1, :, t : t + n] = value

            encode(lambda t: back[k, rows, t : t + TILE], store, RING, FEAT)
            cs_copy(k, j).start()

    def xs_copy(j):
        return remote(xs_s.at[j - 1], xs_r.at[j - 1], xs_sem, (j,), {"col": (c + j) % COLS})

    def sst_copy(j):
        return remote(sst_s, sst_r.at[j - 1], sst_sem, (j,), {"row": (r + j) % ROWS})

    def sct_copy(j):
        return remote(sct_s, sct_r.at[j - 1], sct_sem, (j,), {"col": (c + j) % COLS})

    def last_send():
        for j in range(1, COLS):
            rows = pl.ds(pl.multiple_of(STEP * ((c + j) % COLS), STEP), STEP)

            def store(t, n, value):
                xs_s[j - 1, :, t : t + n] = value

            encode(lambda t: back[LAST, rows, t : t + TILE], store, STEP, FEAT)
            xs_copy(j).start()
        mean_, inv_ = mst[LAST, :, 0:1], mst[LAST, :, 1:2]
        one = jnp.zeros((TOK, 1), f32)
        two = jnp.zeros((TOK, 1), f32)
        for t in range(0, FEAT, 256):
            cols = slice(t, t + 256)
            scaled = back[LAST, :, cols] * gain_row[:, cols]
            centred = (raw[LAST, :, cols].astype(f32) - mean_) * inv_
            one += jnp.sum(scaled, axis=1, keepdims=True)
            two += jnp.sum(scaled * centred, axis=1, keepdims=True)
        lanes = lax.broadcasted_iota(jnp.int32, (TOK, 128), 1)
        sst_s[...] = jnp.where(lanes == 0, one, jnp.where(lanes == 1, two, 0.0)).T[0:8]
        for j in range(1, ROWS):
            sst_copy(j).start()

    def last_stats():
        for j in range(1, ROWS):
            sst_copy(j).wait_recv()
        sct_s[...] = sst_s[...] + sst_r[0] + sst_r[1] + sst_r[2]
        for j in range(1, COLS):
            sct_copy(j).start()

    def last_finish():
        for j in range(1, COLS):
            sct_copy(j).wait_recv()
        sums_ = sct_s[...]
        for j in range(1, COLS):
            sums_ += sct_r[j - 1]
        stt[...] = (jnp.concatenate([sums_, jnp.zeros((120, 128), f32)], axis=0) * count).T
        mine = pl.ds(pl.multiple_of(STEP * c, STEP), STEP)
        one, two = stt[mine, 0:1], stt[mine, 1:2]
        inv_ = mst[LAST, mine, 1:2]
        for j in range(1, COLS):
            xs_copy(j).wait_recv()
        got = [
            decoder(lambda t, n, j=j: xs_r[j - 1, :, t : t + n], FEAT) for j in range(1, COLS)
        ]
        for t in range(0, FEAT, TILE):
            cols = slice(t, t + TILE)
            value = back[LAST, mine, cols]
            for part_ in got:
                value += part_(t)
            input_grad[STEP * LAST : STEP * CHUNKS, cols] = (
                inv_ * (value * gain_row[:, cols] - one - own_centred(LAST, cols) * two)
            ).astype(bf16)

    def lo_copy(k):
        return remote(lo_s.at[k], lo_r.at[k], lo_sem, (k,), {"col": pc})

    def phase_fold(k):
        mine = pl.ds(pl.multiple_of(RING * y, RING), RING)
        for j in range(1, YS):
            cs_copy(k, j).wait_recv()
            got = decoder(lambda t, n: cs_r[k, j - 1, :, t : t + n], FEAT)
            for t in range(0, FEAT, TILE):
                back[k, mine, t : t + TILE] += got(t)
        other = pl.ds(pl.multiple_of(RING * y + STEP * (1 - lo), STEP), STEP)

        def store(t, n, value):
            lo_s[k, :, t : t + n] = value

        encode(lambda t: back[k, other, t : t + TILE], store, STEP, FEAT)
        lo_copy(k).start()

    def gst_copy(k, j):
        return remote(gst_s.at[k], gst_r.at[k, j - 1], gst_sem, (k, j), {"row": (r + j) % ROWS})

    def own_rows(k):
        return pl.ds(pl.multiple_of(STEP * k, STEP), STEP)

    def own_centred(k, cols):
        rows = pl.ds(pl.multiple_of(STEP * c, STEP), STEP)
        return (tok[own_rows(k), cols].astype(f32) - mst[k, rows, 0:1]) * mst[k, rows, 1:2]

    def phase_stats(k):
        lo_copy(k).wait_recv()
        mine = pl.ds(pl.multiple_of(RING * y + STEP * lo, STEP), STEP)
        got = decoder(lambda t, n: lo_r[k, :, t : t + n], FEAT)
        one = jnp.zeros((STEP, 1), f32)
        two = jnp.zeros((STEP, 1), f32)
        for t in range(0, FEAT, TILE):
            cols = slice(t, t + TILE)
            scaled = (back[k, mine, cols] + got(t)) * gain_row[:, cols]
            ng[k, :, cols] = scaled
            one += jnp.sum(scaled, axis=1, keepdims=True)
            two += jnp.sum(scaled * own_centred(k, cols), axis=1, keepdims=True)
        lanes = lax.broadcasted_iota(jnp.int32, (STEP, 128), 1)
        gst_s[k] = jnp.where(lanes == 0, one, jnp.where(lanes == 1, two, 0.0))
        for j in range(1, ROWS):
            gst_copy(k, j).start()

    def phase_finish(k):
        for j in range(1, ROWS):
            gst_copy(k, j).wait_recv()
        sums = (gst_s[k] + gst_r[k, 0] + gst_r[k, 1] + gst_r[k, 2]) * count
        inv_ = mst[k, pl.ds(pl.multiple_of(STEP * c, STEP), STEP), 1:2]
        for t in range(0, FEAT, TILE):
            cols = slice(t, t + TILE)
            input_grad[own_rows(k), cols] = (
                inv_ * (ng[k, :, cols] - sums[:, 0:1] - own_centred(k, cols) * sums[:, 1:2])
            ).astype(bf16)

    def grads_spread():
        up_sum = ugs[d]
        dn_sum = dgs[d]
        for j in range(1, DEPTH):
            ug_copy(j).wait_recv()
            dg_copy(j).wait_recv()
            up_sum += ugr[j]
            dn_sum += dgr[j]
        upx[r] = up_sum
        dnx[c] = dn_sum
        for j in range(1, ROWS):
            ux_copy(j, r).start()
        for j in range(1, COLS):
            dx_copy(j, c).start()

    def drain_early():
        for j in range(1, ROWS):
            stat_copy(j).wait_send()
        for j in range(1, COLS):
            mst_copy(0, j, c).wait_send()
            mst_copy(1, j, c).wait_send()
        for j in range(1, DEPTH):
            dng_copy(j, d).wait_send()
            upg_copy(j, d).wait_send()
        for j in range(1, YS):
            ndiag_copy(j).wait_send()

        def drain_tokens(k, carry):
            for j in range(1, YS):
                nfwd_copy(k, j, pc).wait_send()
            return carry

        def drain(k, carry):
            nlo_copy(k, c).wait_send()
            for j in range(1, YS):
                nown_copy(k, j, c).wait_send()
            for slot in range(6):
                rs_copy(k, slot).wait_send()
            return carry

        lax.fori_loop(0, CHUNKS, drain, 0)
        lax.fori_loop(1, CHUNKS, drain_tokens, 0)

    def iteration(it, carry):
        def step(condition, run):
            pl.when(condition)(run)

        step(it < CHUNKS, lambda: phase_forward(it))

        @pl.when(it == 0)
        def _():
            for k in range(1, CHUNKS):
                forward_tokens(k)

        step((it >= 2) & (it < CHUNKS), lambda: phase_spread(it - 2))
        step(it < CHUNKS, lambda: phase_relay(it))
        step((it >= 1) & (it < CHUNKS + 1), lambda: phase_middle(it - 1))
        step((it >= CHUNKS) & (it < CHUNKS + 2), lambda: phase_spread(it - 2))
        step(it == CHUNKS, up_send)
        step(it == CHUNKS + 2, drain_early)
        step((it >= 3) & (it < CHUNKS + 3), lambda: phase_backward(it - 3))
        step((it >= CHUNKS) & (it < CHUNKS + LAST), lambda: phase_fold(it - CHUNKS))
        step(it >= CHUNKS + 2, lambda: phase_finish(it - CHUNKS - 2))
        step((it > CHUNKS) & (it <= CHUNKS + LAST), lambda: phase_stats(it - CHUNKS - 1))
        step(it == CHUNKS + 2, last_stats)
        step(it == CHUNKS + 2, grads_spread)
        step(it == CHUNKS + 3, last_finish)
        return carry

    lax.fori_loop(0, CHUNKS + LAST + 2, iteration, 0)

    for j in range(1, ROWS):
        ux_copy(j, (r + ROWS - j) % ROWS).wait_recv()
    for j in range(1, COLS):
        dx_copy(j, (c + COLS - j) % COLS).wait_recv()
    up_gradient = upx[0]
    for i in range(1, ROWS):
        up_gradient += upx[i]
    down_gradient = dnx[0]
    for i in range(1, COLS):
        down_gradient += dnx[i]
    up_grad[...] = up_gradient
    down_grad[...] = down_gradient

    for j in range(1, ROWS):
        ux_copy(j, r).wait_send()
    for j in range(1, COLS):
        dx_copy(j, c).wait_send()
    for j in range(1, DEPTH):
        ug_copy(j).wait_send()
        dg_copy(j).wait_send()

    def drain(k, carry):
        for j in range(1, YS):
            cs_copy(k, j).wait_send()
        lo_copy(k).wait_send()
        for j in range(1, ROWS):
            gst_copy(k, j).wait_send()
        return carry

    lax.fori_loop(0, LAST, drain, 0)

    def drain_slopes(k, carry):
        for slot, owner in ((0, r), (1, r), (2, left), (3, r), (4, r), (5, right)):
            ag_copy(k, slot, owner).wait_send()
        return carry

    lax.fori_loop(0, CHUNKS, drain_slopes, 0)
    for j in range(1, ROWS):
        sst_copy(j).wait_send()
    for j in range(1, COLS):
        xs_copy(j).wait_send()
        sct_copy(j).wait_send()


def update_kernel(
    hidden,
    input_grad,
    down_grad,
    up_grad,
    down_w,
    up_w,
    down_m,
    down_s,
    up_m,
    up_s,
    hidden_out,
    input_grad_out,
    new_down_w,
    new_down_m,
    new_down_s,
    new_up_w,
    new_up_m,
    new_up_s,
    sems,
):
    copies = (
        pltpu.make_async_copy(hidden, hidden_out, sems.at[0]),
        pltpu.make_async_copy(input_grad, input_grad_out, sems.at[1]),
    )
    for copy in copies:
        copy.start()
    new_up_w[...], new_up_m[...], new_up_s[...] = adam(
        up_w[...], up_m[...], up_s[...], up_grad[...]
    )
    new_down_w[...], new_down_m[...], new_down_s[...] = adam(
        down_w[...], down_m[...], down_s[...], down_grad[...]
    )
    for copy in copies:
        copy.wait()


def shards(*blocks):
    (tok, w, bias, gain, shift, down_w, up_w, down_m, down_s, up_m, up_s, cot) = blocks
    vmem = pl.BlockSpec(memory_space=pltpu.VMEM)
    hbm = pl.BlockSpec(memory_space=pl.ANY)
    n = CHUNKS
    dma = pltpu.SemaphoreType.DMA
    small = jax.ShapeDtypeStruct((RANK, DNB), f32)
    wide = jax.ShapeDtypeStruct((RANK, UPB), f32)
    scratch = [
        pltpu.VMEM((FEAT, HID), bf16),
        pltpu.VMEM((2 * OWN, HID), bf16),
        dma((2,)),
        pltpu.VMEM((8, 128), f32),
        pltpu.VMEM((ROWS - 1, 8, 128), f32),
        pltpu.VMEM((1, FEAT), f32),
        pltpu.VMEM((1, FEAT), f32),
        pltpu.VMEM((1, HID), f32),
        pltpu.VMEM((n, TOK, FEAT), bf16),
        pltpu.VMEM((n, TOK, 128), f32),
        pltpu.VMEM((n, TOK, FEAT), bf16),
        pltpu.VMEM((DEPTH, RANK, UPB), f32),
        pltpu.VMEM((DEPTH, RANK, DNB), f32),
        pltpu.VMEM((4 * RANK, FEAT), bf16),
        pltpu.VMEM((4 * RANK, FEAT), bf16),
        pltpu.VMEM((4 * RANK, HID), bf16),
        pltpu.VMEM((4 * RANK, HID), bf16),
        pltpu.VMEM((n, TOK, HID + 128), f32),
        pltpu.VMEM((n, TOK, 4 * RANK), bf16),
        pltpu.VMEM((n, 6, STEP, HID + 128), bf16),
        pltpu.VMEM((n, 6, STEP, HID + 128), bf16),
        pltpu.VMEM((n, TOK, HID), bf16),
        pltpu.VMEM((n, TOK, FEAT), f32),
        pltpu.VMEM((LAST, YS - 1, RING, FEAT + 128), bf16),
        pltpu.VMEM((LAST, YS - 1, RING, FEAT + 128), bf16),
        pltpu.VMEM((LAST, STEP, FEAT + 128), bf16),
        pltpu.VMEM((LAST, STEP, FEAT + 128), bf16),
        pltpu.VMEM((LAST, STEP, FEAT), f32),
        pltpu.VMEM((LAST, STEP, 128), f32),
        pltpu.VMEM((LAST, ROWS - 1, STEP, 128), f32),
        pltpu.VMEM((COLS - 1, STEP, FEAT + 128), bf16),
        pltpu.VMEM((COLS - 1, STEP, FEAT + 128), bf16),
        pltpu.VMEM((8, 128), f32),
        pltpu.VMEM((ROWS - 1, 8, 128), f32),
        pltpu.VMEM((8, 128), f32),
        pltpu.VMEM((COLS - 1, 8, 128), f32),
        pltpu.VMEM((TOK, 128), f32),
        pltpu.VMEM((n, RING, 128), f32),
        pltpu.VMEM((RANK, FEAT), f32),
        pltpu.VMEM((DEPTH, RANK, UPB), f32),
        pltpu.VMEM((DEPTH, RANK, UPB), f32),
        pltpu.VMEM((DEPTH, RANK, DNB), f32),
        pltpu.VMEM((DEPTH, RANK, DNB), f32),
        pltpu.VMEM((ROWS, RANK, UPB), f32),
        pltpu.VMEM((COLS, RANK, DNB), f32),
        dma((2, ROWS)),
        dma((2, 2, COLS)),
        dma((2, n)),
        dma((2, n, YS)),
        dma((2, n, YS)),
        dma((2, DEPTH)),
        dma((2, DEPTH)),
        dma((2, n, 6)),
        dma((2, n, 6)),
        dma((2, LAST, YS)),
        dma((2, LAST)),
        dma((2, LAST, ROWS)),
        dma((2, COLS)),
        dma((2, ROWS)),
        dma((2, COLS)),
        dma((2, DEPTH)),
        dma((2, DEPTH)),
        dma((2, ROWS)),
        dma((2, COLS)),
    ]
    outs = pl.pallas_call(
        kernel,
        out_shape=(
            jax.ShapeDtypeStruct((2 * OWN, HID), bf16),
            jax.ShapeDtypeStruct((OWN, FEAT), bf16),
            small,
            wide,
        ),
        in_specs=[vmem, hbm] + [vmem] * 5 + [hbm],
        out_specs=(vmem,) * 4,
        scratch_shapes=scratch,
        compiler_params=pltpu.CompilerParams(
            collective_id=0, has_side_effects=True, vmem_limit_bytes=56 * 1024 * 1024
        ),
        cost_estimate=pl.CostEstimate(
            flops=4 * 512 * FEAT * HID, bytes_accessed=14000000, transcendentals=10000000
        ),
        name="fused_step",
    )(tok, w, bias, gain, shift, down_w, up_w, cot)
    return pl.pallas_call(
        update_kernel,
        out_shape=(
            jax.ShapeDtypeStruct((2 * OWN, HID), bf16),
            jax.ShapeDtypeStruct((OWN, FEAT), bf16),
            small,
            small,
            small,
            wide,
            wide,
            wide,
        ),
        in_specs=[vmem] * 10,
        out_specs=(hbm, hbm) + (vmem,) * 6,
        scratch_shapes=[dma((2,))],
        name="adapter_update",
    )(*outs, down_w, up_w, down_m, down_s, up_m, up_s)


def solution(mesh):
    down = P(None, ("row", "depth"))
    up = P(None, ("col", "depth"))
    return jax.shard_map(
        shards,
        mesh=mesh,
        in_specs=(
            P(("depth", "col"), "row"),
            P("row", "col"),
            P("col"),
            P("row"),
            P("row"),
            down,
            up,
            down,
            down,
            up,
            up,
            P(("depth", "row"), "col"),
        ),
        out_specs=(
            P(("depth", "row"), "col"),
            P(("depth", "col"), "row"),
            down,
            down,
            down,
            up,
            up,
            up,
        ),
        check_vma=False,
    )
```

```python
import functools
import jax
import jax.numpy as jnp
from jax import lax
from jax.experimental import pallas as pl
from jax.experimental.pallas import tpu as pltpu
from jax.sharding import PartitionSpec as P

adapter_scale = 0.5
norm_epsilon = 1e-05
beta_first = 0.9
beta_second = 0.999
adam_step = 10
learn_rate = 0.01
decay_rate = 0.1
adam_epsilon = 1e-08

f32 = jnp.float32
bf16 = jnp.bfloat16
MESH = pl.DeviceIdType.MESH
NT = (((1,), (1,)), ((), ()))

ROWS, COLS, DEPTH = 4, 8, 8
YS = COLS // 2
CHUNKS = 4
OWN = 64
STEP = OWN // CHUNKS
TOK = STEP * COLS
FEAT, HID, RANK = 1536, 3072, 32
UPB, DNB = HID // DEPTH, FEAT // DEPTH
RING = 2 * STEP
CODE_SPAN = 120.0
LN2 = 0.6931471805599453
TILE = 512
WIDE = 1024
HALF = FEAT // 2
LAST = CHUNKS - 1


def gelu_both(v):
    inner = 0.7978845608 * (v + 0.044715 * v * v * v)
    tangent = jnp.tanh(inner)
    value = 0.5 * v * (1.0 + tangent)
    slope = 0.5 * (1.0 + tangent) + 0.5 * v * (1.0 - tangent * tangent) * 0.7978845608 * (
        1.0 + 3.0 * 0.044715 * v * v
    )
    return value, slope


def adam(weight, moment, square, gradient):
    new_moment = beta_first * moment + (1.0 - beta_first) * gradient
    new_square = beta_second * square + (1.0 - beta_second) * gradient * gradient
    update = (
        new_moment
        / (1.0 - beta_first**adam_step)
        / (jnp.sqrt(new_square / (1.0 - beta_second**adam_step)) + adam_epsilon)
    )
    return weight - learn_rate * (update + decay_rate * weight), new_moment, new_square


def encode(load, store, rows, width, tile=TILE):
    top = jnp.zeros((rows, 1), f32)
    for t in range(0, width, tile):
        top = jnp.maximum(top, jnp.max(jnp.abs(load(t)), axis=1, keepdims=True))
    top = (jnp.maximum(top, 1e-30) * 1.01).astype(bf16)
    factor = CODE_SPAN / top.astype(f32)
    for t in range(0, width, tile):
        store(t, tile, jnp.exp2(load(t) * factor).astype(bf16))
    store(width, 128, jnp.broadcast_to(top, (rows, 128)))


def decoder(load, width, tile=TILE):
    scale = load(width, 128)[:, 0:1].astype(f32) * (1.0 / (CODE_SPAN * LN2))
    return lambda t: jnp.log(load(t, tile).astype(f32)) * scale


def kernel(
    tok,
    w_hbm,
    bias,
    gain,
    shift,
    down_w,
    up_w,
    cot_hbm,
    hidden,
    input_grad,
    down_grad,
    up_grad,
    w,
    cot,
    local_sem,
    hid,
    stat_s,
    stat_r,
    gain_row,
    shift_row,
    bias_row,
    raw,
    mst,
    nrm,
    upg,
    dng,
    d_low,
    d_prod,
    u_low,
    u_prod,
    part,
    low,
    rs_s,
    rs_r,
    slg,
    back,
    cs_s,
    cs_r,
    lo_s,
    lo_r,
    ng,
    gst_s,
    gst_r,
    xs_s,
    xs_r,
    sst_s,
    sst_r,
    sct_s,
    sct_r,
    stt,
    low_own,
    dn_acc,
    ugs,
    ugr,
    dgs,
    dgr,
    upx,
    dnx,
    stat_sem,
    mst_sem,
    nlo_sem,
    nown_sem,
    nfwd_sem,
    upg_sem,
    dng_sem,
    rs_sem,
    ag_sem,
    cs_sem,
    lo_sem,
    gst_sem,
    xs_sem,
    sst_sem,
    sct_sem,
    ug_sem,
    dg_sem,
    ux_sem,
    dx_sem,
):
    r = lax.axis_index("row")
    c = lax.axis_index("col")
    d = lax.axis_index("depth")
    y, lo = c // 2, c % 2
    right, left, opp = (r + 1) % ROWS, (r + 3) % ROWS, (r + 2) % ROWS
    pc = y * 2 + (1 - lo)

    def remote(src, dst, sems, index, device):
        return pltpu.make_async_remote_copy(
            src_ref=src,
            dst_ref=dst,
            send_sem=sems.at[(0,) + index],
            recv_sem=sems.at[(1,) + index],
            device_id=device,
            device_id_type=MESH,
        )

    w_copy = pltpu.make_async_copy(w_hbm, w, local_sem.at[0])
    cot_copy = pltpu.make_async_copy(cot_hbm, cot, local_sem.at[1])
    hid_copy = pltpu.make_async_copy(hid, hidden, local_sem.at[2])
    w_copy.start()
    cot_copy.start()

    barrier = pltpu.get_barrier_semaphore()
    for j in range(1, ROWS):
        pl.semaphore_signal(barrier, inc=1, device_id={"row": (r + j) % ROWS}, device_id_type=MESH)
    for j in range(1, COLS):
        pl.semaphore_signal(barrier, inc=1, device_id={"col": (c + j) % COLS}, device_id_type=MESH)
    for j in range(1, DEPTH):
        pl.semaphore_signal(
            barrier, inc=1, device_id={"depth": (d + j) % DEPTH}, device_id_type=MESH
        )

    x = tok[...].astype(f32)
    lane = lax.broadcasted_iota(jnp.int32, (OWN, 128), 1)
    s1 = jnp.sum(x, axis=1, keepdims=True)
    s2 = jnp.sum(x * x, axis=1, keepdims=True)
    sums = jnp.where(lane == 0, s1, jnp.where(lane == 1, s2, 0.0))
    stat_s[...] = jnp.concatenate([sums, jnp.zeros_like(sums)], axis=0).T[0:8]
    upg[d] = up_w[...]
    dng[d] = down_w[...]
    for k in range(CHUNKS):
        raw[k, pl.ds(pl.multiple_of(STEP * c, STEP), STEP), :] = tok[STEP * k : STEP * (k + 1), :]
    pl.semaphore_wait(barrier, ROWS + COLS + DEPTH - 3)

    def stat_copy(j):
        return remote(stat_s, stat_r.at[j - 1], stat_sem, (j,), {"row": (r + j) % ROWS})

    def upg_copy(j, owner):
        return remote(upg.at[owner], upg.at[owner], upg_sem, (j,), {"depth": (d + j) % DEPTH})

    def dng_copy(j, owner):
        return remote(dng.at[owner], dng.at[owner], dng_sem, (j,), {"depth": (d + j) % DEPTH})

    for j in range(1, ROWS):
        stat_copy(j).start()

    def token_rows(k, col):
        return raw.at[k, pl.ds(pl.multiple_of(STEP * col, STEP), STEP)]

    def nlo_copy(k, col):
        return remote(token_rows(k, col), token_rows(k, col), nlo_sem, (k,), {"col": pc})

    def y_peer(j):
        return {"col": ((y + j) % YS) * 2 + lo}

    def nown_copy(k, j, col):
        return remote(token_rows(k, col), token_rows(k, col), nown_sem, (k, j), y_peer(j))

    def nfwd_copy(k, j, col):
        return remote(token_rows(k, col), token_rows(k, col), nfwd_sem, (k, j), y_peer(j))

    def ndiag_copy(j):
        peer = {"col": ((y + j) % YS) * 2 + (1 - lo)}
        return remote(token_rows(0, c), token_rows(0, c), nfwd_sem, (0, j), peer)

    for j in range(1, YS):
        ndiag_copy(j).start()
        nown_copy(0, j, c).start()

    nlo_copy(0, c).start()
    for j in range(1, DEPTH):
        dng_copy(j, d).start()
    for j in range(1, DEPTH):
        upg_copy(j, d).start()

    def forward_tokens(k):
        nlo_copy(k, pc).wait_recv()
        for j in range(1, YS):
            nfwd_copy(k, j, pc).start()

    gain_row[...] = gain[...].astype(f32).reshape(1, FEAT)
    shift_row[...] = shift[...].astype(f32).reshape(1, FEAT)
    bias_row[...] = bias[...].astype(f32).reshape(1, HID)
    for j in range(1, ROWS):
        stat_copy(j).wait_recv()
    total = stat_s[...] + stat_r[0] + stat_r[1] + stat_r[2]
    total = jnp.concatenate([total, jnp.zeros((120, 128), f32)], axis=0).T[0:OWN]
    count = 1.0 / (FEAT * ROWS)
    mean = total[:, 0:1] * count
    inv = lax.rsqrt(total[:, 1:2] * count - mean * mean + norm_epsilon)
    both = jnp.where(lane == 0, mean, inv)
    for k in range(CHUNKS):
        mst[k, pl.ds(pl.multiple_of(STEP * c, STEP), STEP), :] = both[STEP * k : STEP * (k + 1)]

    def mst_copy(late, j, col):
        rows = pl.ds(pl.multiple_of(STEP * col, STEP), STEP)
        ref = mst.at[pl.ds(1, CHUNKS - 1), rows] if late else mst.at[0, rows]
        return remote(ref, ref, mst_sem, (late, j), {"col": (c + j) % COLS})

    for late in (0, 1):
        for j in range(1, COLS):
            mst_copy(late, j, c).start()

    def send_own(k, carry):
        nlo_copy(k, c).start()
        for j in range(1, YS):
            nown_copy(k, j, c).start()
        return carry

    lax.fori_loop(1, CHUNKS, send_own, 0)

    def adapter_operands():
        for j in range(1, DEPTH):
            dng_copy(j, (d + DEPTH - j) % DEPTH).wait_recv()
        for i in range(DEPTH // 2):
            u = jnp.concatenate([dng[2 * i], dng[2 * i + 1]], axis=1)
            high = u.astype(bf16)
            mid_part = (u - high.astype(f32)).astype(bf16)
            zero = jnp.zeros_like(high)
            cols = slice(2 * DNB * i, 2 * DNB * (i + 1))
            d_low[:, cols] = jnp.concatenate([high, high, high, zero], axis=0)
            d_prod[:, cols] = jnp.concatenate([high, mid_part, high, zero], axis=0)
        for j in range(1, DEPTH):
            upg_copy(j, (d + DEPTH - j) % DEPTH).wait_recv()
        for i in range(DEPTH):
            u = upg[i]
            high = u.astype(bf16)
            mid_part = (u - high.astype(f32)).astype(bf16)
            zero = jnp.zeros_like(high)
            cols = slice(UPB * i, UPB * (i + 1))
            u_low[:, cols] = jnp.concatenate([high, high, high, zero], axis=0)
            u_prod[:, cols] = jnp.concatenate([high, mid_part, high, zero], axis=0)

    dn_acc[...] = jnp.zeros_like(dn_acc)
    w_copy.wait()
    cot_copy.wait()

    def split(value):
        high = value.astype(bf16).astype(f32)
        lanes = lax.broadcasted_iota(jnp.int32, value.shape, 1)
        return jnp.where(lanes < 2 * RANK, high, value - high).astype(bf16)

    def part_rows(k, owner, half):
        start = pl.multiple_of(RING * owner + STEP * half, STEP)
        return k, pl.ds(start, STEP)

    def rs_copy(k, slot):
        target = right if slot < 3 else left
        return remote(rs_s.at[k, slot], rs_r.at[k, slot], rs_sem, (k, slot), {"row": target})

    tail = lax.broadcasted_iota(jnp.int32, (STEP, 128), 1)

    def rs_decoder(k, slot):
        last = rs_r[k, slot, :, HID : HID + 128].astype(f32) * 1.0
        main = decoder(
            lambda t, n: last[:, 64:128] if t == HID else rs_r[k, slot, :, t : t + n], HID
        )
        scale = last[:, 96:97] * (1.0 / (CODE_SPAN * LN2))
        return main, jnp.where(tail < 2 * RANK, jnp.log(last) * scale, 0.0)

    def rs_send(k, slot, owner, half):
        kk, rows = part_rows(k, owner, half)
        value = part[kk, rows, HID : HID + 128]
        top = jnp.max(jnp.abs(value), axis=1, keepdims=True)
        top = (jnp.maximum(top, 1e-30) * 1.01).astype(bf16).astype(f32)
        code = jnp.exp2(value * (CODE_SPAN / top))

        def store(t, n, coded):
            if t == HID:
                scale = jnp.where(tail < 3 * RANK, coded.astype(f32), top)
                coded = jnp.where(tail < 2 * RANK, code, scale).astype(bf16)
            rs_s[k, slot, :, t : t + n] = coded

        encode(lambda t: part[kk, rows, t : t + TILE], store, STEP, HID)
        rs_copy(k, slot).start()

    def phase_forward(k):
        @pl.when(k == 0)
        def _():
            nlo_copy(0, pc).wait_recv()
            for j in range(1, COLS):
                mst_copy(0, j, (c + COLS - j) % COLS).wait_recv()

        @pl.when(k == 1)
        def _():
            for j in range(1, COLS):
                mst_copy(1, j, (c + COLS - j) % COLS).wait_recv()

        for j in range(1, YS):
            source = (y + YS - j) % YS
            nown_copy(k, j, source * 2 + lo).wait_recv()
            nfwd_copy(k, j, source * 2 + (1 - lo)).wait_recv()
        mean_, inv_ = mst[k, :, 0:1], mst[k, :, 1:2]
        for t in range(0, FEAT, TILE):
            cols = slice(t, t + TILE)
            nrm[k, :, cols] = (
                (raw[k, :, cols].astype(f32) - mean_) * inv_ * gain_row[:, cols]
                + shift_row[:, cols]
            ).astype(bf16)
        def rank_product():
            value = adapter_scale * lax.dot_general(
                nrm[k], d_low[...], NT, preferred_element_type=f32
            )
            part[k, :, HID : HID + 128] = value
            low[k] = split(value)

        def rank_tile(cols):
            return jnp.dot(low[k], u_prod[:, cols], preferred_element_type=f32)

        def columns(t):
            return pl.ds(pl.multiple_of(t * WIDE, WIDE), WIDE)

        def main_tile(cols):
            return jnp.dot(nrm[k], w[:, cols], preferred_element_type=f32)

        @pl.when(k == 0)
        def _():
            def tile(t, carry):
                part[k, :, columns(t)] = main_tile(columns(t))
                return carry

            def add(t, carry):
                part[k, :, columns(t)] += rank_tile(columns(t))
                return carry

            lax.fori_loop(0, HID // WIDE, tile, 0)
            adapter_operands()
            rank_product()
            lax.fori_loop(0, HID // WIDE, add, 0)

        @pl.when(k > 0)
        def _():
            def tile(t, carry):
                part[k, :, columns(t)] = main_tile(columns(t)) + rank_tile(columns(t))
                return carry

            rank_product()
            lax.fori_loop(0, HID // WIDE, tile, 0)

        rs_send(k, 0, opp, 0)
        rs_send(k, 3, opp, 1)
        rs_send(k, 1, right, 1)
        rs_send(k, 4, left, 0)

    def phase_relay(k):
        for slot, owner, half in ((0, right, 0), (3, left, 1)):
            rs_copy(k, slot).wait_recv()
            kk, rows = part_rows(k, owner, half)
            got, low_got = rs_decoder(k, slot)
            part[kk, rows, HID : HID + 128] += low_got
            for t in range(0, HID, TILE):
                part[kk, rows, t : t + TILE] += got(t)
            rs_send(k, slot + 2, owner, half)

    def slope_rows(k, owner, first, count_):
        return slg.at[k, pl.ds(pl.multiple_of(RING * owner + first, STEP), count_)]

    ag_half = (0, 1, 0, 1, 0, 1)

    def ag_copy(k, slot, owner):
        rows = slope_rows(k, owner, STEP * ag_half[slot], STEP)
        target = right if slot < 3 else left
        return remote(rows, rows, ag_sem, (k, slot), {"row": target})

    def phase_middle(k):
        for half, first, second in ((0, 4, 2), (1, 1, 5)):
            rs_copy(k, first).wait_recv()
            rs_copy(k, second).wait_recv()
            kk, rows = part_rows(k, r, half)
            (one, low_one), (two, low_two) = rs_decoder(k, first), rs_decoder(k, second)
            low_own[k, STEP * half : STEP * (half + 1), :] = (
                part[kk, rows, HID : HID + 128] + low_one + low_two
            )
            start = pl.multiple_of(OWN * half + STEP * k, STEP)
            for t in range(0, HID, TILE):
                cols = slice(t, t + TILE)
                v = part[kk, rows, cols] + one(t) + two(t) + bias_row[:, cols]
                value, slope = gelu_both(v)
                hid[pl.ds(start, STEP), cols] = value.astype(bf16)
                slg[kk, rows, cols] = (
                    cot[pl.ds(start, STEP), cols].astype(f32) * slope
                ).astype(bf16)
            for slot in (0,) if half == 0 else (3, 1, 4):
                ag_copy(k, slot, r).start()

    def phase_spread(k):
        ag_copy(k, 0, left).wait_recv()
        ag_copy(k, 2, left).start()
        ag_copy(k, 3, right).wait_recv()
        ag_copy(k, 5, right).start()

    def cs_copy(k, j):
        return remote(cs_s.at[k, j - 1], cs_r.at[k, j - 1], cs_sem, (k, j), y_peer(j))

    def ug_copy(j):
        peer = (d + j) % DEPTH
        return remote(ugs.at[peer], ugr.at[j], ug_sem, (j,), {"depth": peer})

    def dg_copy(j):
        peer = (d + j) % DEPTH
        return remote(dgs.at[peer], dgr.at[j], dg_sem, (j,), {"depth": peer})

    def ux_copy(j, owner):
        return remote(upx.at[owner], upx.at[owner], ux_sem, (j,), {"row": (r + j) % ROWS})

    def dx_copy(j, owner):
        return remote(dnx.at[owner], dnx.at[owner], dx_sem, (j,), {"col": (c + j) % COLS})

    def down_send():
        for i in range(DEPTH):
            dgs[i] = dn_acc[:, DNB * i : DNB * (i + 1)]
        for j in range(1, DEPTH):
            dg_copy(j).start()

    def up_send():
        hid_copy.start()
        lanes = lax.broadcasted_iota(jnp.int32, (RING, 128), 1)
        sides = []
        for k in range(CHUNKS):
            value = low_own[k]
            high = value.astype(bf16).astype(f32)
            both_parts = jnp.where(
                lanes < RANK, high, jnp.where(lanes < 2 * RANK, value - high, 0.0)
            )
            sides.append(both_parts.T.astype(bf16))
        for i in range(DEPTH):
            cols = slice(UPB * i, UPB * (i + 1))
            g = jnp.zeros((128, UPB), f32)
            for k in range(CHUNKS):
                rows = pl.ds(pl.multiple_of(RING * r, RING), RING)
                g += jnp.dot(sides[k], slg[k, rows, cols], preferred_element_type=f32)
            ugs[i] = g[0:RANK] + g[RANK : 2 * RANK]
        for j in range(1, DEPTH):
            ug_copy(j).start()

    def phase_backward(k):
        ag_copy(k, 1, left).wait_recv()
        ag_copy(k, 4, right).wait_recv()
        ag_copy(k, 2, opp).wait_recv()
        ag_copy(k, 5, opp).wait_recv()
        slopes = slg[k]
        rank = split(
            adapter_scale * lax.dot_general(slopes, u_low[...], NT, preferred_element_type=f32)
        )
        rank_t = rank.astype(f32).T.astype(bf16)

        def grow_down(t, carry):
            cols = pl.ds(pl.multiple_of(t * TILE, TILE), TILE)
            g = jnp.dot(rank_t, nrm[k, :, cols], preferred_element_type=f32)
            dn_acc[:, cols] += g[0:RANK] + g[2 * RANK : 3 * RANK]
            return carry

        lax.fori_loop(0, FEAT // TILE, grow_down, 0)

        @pl.when(k == CHUNKS - 1)
        def _():
            down_send()

        bsize = HALF

        def tile(t, carry):
            rows = pl.ds(pl.multiple_of(t * bsize, bsize), bsize)
            back[k, :, rows] = lax.dot_general(
                slg[k], w[rows, :], NT, preferred_element_type=f32
            ) + jnp.dot(rank, d_prod[:, rows], preferred_element_type=f32)
            return carry

        @pl.when(k < LAST)
        def _():
            lax.fori_loop(0, FEAT // bsize, tile, 0)
            fold_send(k)

        @pl.when(k == LAST)
        def _():
            def both_steps(half, carry):
                tile(half, carry)
                last_send(half)
                return carry

            lax.fori_loop(0, FEAT // bsize, both_steps, 0)
            last_sums()

    def fold_send(k):
        for j in range(1, YS):
            rows = pl.ds(pl.multiple_of(RING * ((y + j) % YS), RING), RING)

            def store(t, n, value):
                cs_s[k, j - 1, :, t : t + n] = value

            encode(lambda t: back[k, rows, t : t + TILE], store, RING, FEAT)
            cs_copy(k, j).start()

    def xs_copy(half, j):
        return remote(
            xs_s.at[half, j - 1],
            xs_r.at[half, j - 1],
            xs_sem,
            (half, j),
            {"col": (c + j) % COLS},
        )

    def sst_copy(j):
        return remote(sst_s, sst_r.at[j - 1], sst_sem, (j,), {"row": (r + j) % ROWS})

    def sct_copy(j):
        return remote(sct_s, sct_r.at[j - 1], sct_sem, (j,), {"col": (c + j) % COLS})

    def last_send(half):
        for j in range(1, COLS):
            rows = pl.ds(pl.multiple_of(STEP * ((c + j) % COLS), STEP), STEP)

            def load(t):
                return back[LAST, rows, pl.ds(pl.multiple_of(HALF * half + t, 256), 256)]

            def store(t, n, value):
                xs_s[half, j - 1, :, t : t + n] = value

            encode(load, store, STEP, HALF, 256)
            xs_copy(half, j).start()

    def last_sums():
        mean_, inv_ = mst[LAST, :, 0:1], mst[LAST, :, 1:2]
        one = jnp.zeros((TOK, 1), f32)
        two = jnp.zeros((TOK, 1), f32)
        for t in range(0, FEAT, 256):
            cols = slice(t, t + 256)
            scaled = back[LAST, :, cols] * gain_row[:, cols]
            centred = (raw[LAST, :, cols].astype(f32) - mean_) * inv_
            one += jnp.sum(scaled, axis=1, keepdims=True)
            two += jnp.sum(scaled * centred, axis=1, keepdims=True)
        lanes = lax.broadcasted_iota(jnp.int32, (TOK, 128), 1)
        sst_s[...] = jnp.where(lanes == 0, one, jnp.where(lanes == 1, two, 0.0)).T[0:8]
        for j in range(1, ROWS):
            sst_copy(j).start()

    def last_stats():
        for j in range(1, ROWS):
            sst_copy(j).wait_recv()
        sct_s[...] = sst_s[...] + sst_r[0] + sst_r[1] + sst_r[2]
        for j in range(1, COLS):
            sct_copy(j).start()

    def last_finish():
        for j in range(1, COLS):
            sct_copy(j).wait_recv()
        sums_ = sct_s[...]
        for j in range(1, COLS):
            sums_ += sct_r[j - 1]
        stt[...] = (jnp.concatenate([sums_, jnp.zeros((120, 128), f32)], axis=0) * count).T
        mine = pl.ds(pl.multiple_of(STEP * c, STEP), STEP)
        one, two = stt[mine, 0:1], stt[mine, 1:2]
        inv_ = mst[LAST, mine, 1:2]
        for half in range(2):
            for j in range(1, COLS):
                xs_copy(half, j).wait_recv()
            got = [
                decoder(lambda t, n, j=j: xs_r[half, j - 1, :, t : t + n], HALF, 256)
                for j in range(1, COLS)
            ]
            for t in range(0, HALF, 256):
                cols = slice(HALF * half + t, HALF * half + t + 256)
                value = back[LAST, mine, cols]
                for part_ in got:
                    value += part_(t)
                input_grad[STEP * LAST : STEP * CHUNKS, cols] = (
                    inv_ * (value * gain_row[:, cols] - one - own_centred(LAST, cols) * two)
                ).astype(bf16)

    def lo_copy(k):
        return remote(lo_s.at[k], lo_r.at[k], lo_sem, (k,), {"col": pc})

    def phase_fold(k):
        mine = pl.ds(pl.multiple_of(RING * y, RING), RING)
        for j in range(1, YS):
            cs_copy(k, j).wait_recv()
            got = decoder(lambda t, n: cs_r[k, j - 1, :, t : t + n], FEAT)
            for t in range(0, FEAT, TILE):
                back[k, mine, t : t + TILE] += got(t)
        other = pl.ds(pl.multiple_of(RING * y + STEP * (1 - lo), STEP), STEP)

        def store(t, n, value):
            lo_s[k, :, t : t + n] = value

        encode(lambda t: back[k, other, t : t + TILE], store, STEP, FEAT)
        lo_copy(k).start()

    def gst_copy(k, j):
        return remote(gst_s.at[k], gst_r.at[k, j - 1], gst_sem, (k, j), {"row": (r + j) % ROWS})

    def own_rows(k):
        return pl.ds(pl.multiple_of(STEP * k, STEP), STEP)

    def own_centred(k, cols):
        rows = pl.ds(pl.multiple_of(STEP * c, STEP), STEP)
        return (tok[own_rows(k), cols].astype(f32) - mst[k, rows, 0:1]) * mst[k, rows, 1:2]

    def phase_stats(k):
        lo_copy(k).wait_recv()
        mine = pl.ds(pl.multiple_of(RING * y + STEP * lo, STEP), STEP)
        got = decoder(lambda t, n: lo_r[k, :, t : t + n], FEAT)
        one = jnp.zeros((STEP, 1), f32)
        two = jnp.zeros((STEP, 1), f32)
        for t in range(0, FEAT, TILE):
            cols = slice(t, t + TILE)
            scaled = (back[k, mine, cols] + got(t)) * gain_row[:, cols]
            ng[k, :, cols] = scaled
            one += jnp.sum(scaled, axis=1, keepdims=True)
            two += jnp.sum(scaled * own_centred(k, cols), axis=1, keepdims=True)
        lanes = lax.broadcasted_iota(jnp.int32, (STEP, 128), 1)
        gst_s[k] = jnp.where(lanes == 0, one, jnp.where(lanes == 1, two, 0.0))
        for j in range(1, ROWS):
            gst_copy(k, j).start()

    def phase_finish(k):
        for j in range(1, ROWS):
            gst_copy(k, j).wait_recv()
        sums = (gst_s[k] + gst_r[k, 0] + gst_r[k, 1] + gst_r[k, 2]) * count
        inv_ = mst[k, pl.ds(pl.multiple_of(STEP * c, STEP), STEP), 1:2]
        for t in range(0, FEAT, TILE):
            cols = slice(t, t + TILE)
            input_grad[own_rows(k), cols] = (
                inv_ * (ng[k, :, cols] - sums[:, 0:1] - own_centred(k, cols) * sums[:, 1:2])
            ).astype(bf16)

    def grads_spread():
        up_sum = ugs[d]
        dn_sum = dgs[d]
        for j in range(1, DEPTH):
            ug_copy(j).wait_recv()
            dg_copy(j).wait_recv()
            up_sum += ugr[j]
            dn_sum += dgr[j]
        upx[r] = up_sum
        dnx[c] = dn_sum
        for j in range(1, ROWS):
            ux_copy(j, r).start()
        for j in range(1, COLS):
            dx_copy(j, c).start()

    def drain_early():
        for j in range(1, ROWS):
            stat_copy(j).wait_send()
        for j in range(1, COLS):
            mst_copy(0, j, c).wait_send()
            mst_copy(1, j, c).wait_send()
        for j in range(1, DEPTH):
            dng_copy(j, d).wait_send()
            upg_copy(j, d).wait_send()
        for j in range(1, YS):
            ndiag_copy(j).wait_send()

        def drain_tokens(k, carry):
            for j in range(1, YS):
                nfwd_copy(k, j, pc).wait_send()
            return carry

        def drain(k, carry):
            nlo_copy(k, c).wait_send()
            for j in range(1, YS):
                nown_copy(k, j, c).wait_send()
            for slot in range(6):
                rs_copy(k, slot).wait_send()
            return carry

        lax.fori_loop(0, CHUNKS, drain, 0)
        lax.fori_loop(1, CHUNKS, drain_tokens, 0)

    def iteration(it, carry):
        def step(condition, run):
            pl.when(condition)(run)

        step(it < CHUNKS, lambda: phase_forward(it))

        @pl.when(it == 0)
        def _():
            for k in range(1, CHUNKS):
                forward_tokens(k)

        step((it >= 2) & (it < CHUNKS), lambda: phase_spread(it - 2))
        step(it < CHUNKS, lambda: phase_relay(it))
        step((it >= 1) & (it < CHUNKS + 1), lambda: phase_middle(it - 1))
        step((it >= CHUNKS) & (it < CHUNKS + 2), lambda: phase_spread(it - 2))
        step(it == CHUNKS, up_send)
        step(it == CHUNKS + 2, drain_early)
        step((it >= 3) & (it < CHUNKS + 3), lambda: phase_backward(it - 3))
        step((it >= CHUNKS) & (it < CHUNKS + LAST), lambda: phase_fold(it - CHUNKS))
        step(it >= CHUNKS + 2, lambda: phase_finish(it - CHUNKS - 2))
        step((it > CHUNKS) & (it <= CHUNKS + LAST), lambda: phase_stats(it - CHUNKS - 1))
        step(it == CHUNKS + 2, last_stats)
        step(it == CHUNKS + 2, grads_spread)
        step(it == CHUNKS + 3, last_finish)
        return carry

    lax.fori_loop(0, CHUNKS + LAST + 2, iteration, 0)

    for j in range(1, ROWS):
        ux_copy(j, (r + ROWS - j) % ROWS).wait_recv()
    for j in range(1, COLS):
        dx_copy(j, (c + COLS - j) % COLS).wait_recv()
    up_gradient = upx[0]
    for i in range(1, ROWS):
        up_gradient += upx[i]
    down_gradient = dnx[0]
    for i in range(1, COLS):
        down_gradient += dnx[i]
    up_grad[...] = up_gradient
    down_grad[...] = down_gradient

    hid_copy.wait()
    for j in range(1, ROWS):
        ux_copy(j, r).wait_send()
    for j in range(1, COLS):
        dx_copy(j, c).wait_send()
    for j in range(1, DEPTH):
        ug_copy(j).wait_send()
        dg_copy(j).wait_send()

    def drain(k, carry):
        for j in range(1, YS):
            cs_copy(k, j).wait_send()
        lo_copy(k).wait_send()
        for j in range(1, ROWS):
            gst_copy(k, j).wait_send()
        return carry

    lax.fori_loop(0, LAST, drain, 0)

    def drain_slopes(k, carry):
        for slot, owner in ((0, r), (1, r), (2, left), (3, r), (4, r), (5, right)):
            ag_copy(k, slot, owner).wait_send()
        return carry

    lax.fori_loop(0, CHUNKS, drain_slopes, 0)
    for j in range(1, ROWS):
        sst_copy(j).wait_send()
    for j in range(1, COLS):
        xs_copy(0, j).wait_send()
        xs_copy(1, j).wait_send()
        sct_copy(j).wait_send()


def update_kernel(
    hidden,
    input_grad,
    down_grad,
    up_grad,
    down_w,
    up_w,
    down_m,
    down_s,
    up_m,
    up_s,
    hidden_out,
    input_grad_out,
    new_down_w,
    new_down_m,
    new_down_s,
    new_up_w,
    new_up_m,
    new_up_s,
    sems,
):
    copies = (
        pltpu.make_async_copy(hidden, hidden_out, sems.at[0]),
        pltpu.make_async_copy(input_grad, input_grad_out, sems.at[1]),
    )
    for copy in copies:
        copy.start()
    new_up_w[...], new_up_m[...], new_up_s[...] = adam(
        up_w[...], up_m[...], up_s[...], up_grad[...]
    )
    new_down_w[...], new_down_m[...], new_down_s[...] = adam(
        down_w[...], down_m[...], down_s[...], down_grad[...]
    )
    for copy in copies:
        copy.wait()


def shards(*blocks):
    (tok, w, bias, gain, shift, down_w, up_w, down_m, down_s, up_m, up_s, cot) = blocks
    vmem = pl.BlockSpec(memory_space=pltpu.VMEM)
    hbm = pl.BlockSpec(memory_space=pl.ANY)
    n = CHUNKS
    dma = pltpu.SemaphoreType.DMA
    small = jax.ShapeDtypeStruct((RANK, DNB), f32)
    wide = jax.ShapeDtypeStruct((RANK, UPB), f32)
    scratch = [
        pltpu.VMEM((FEAT, HID), bf16),
        pltpu.VMEM((2 * OWN, HID), bf16),
        dma((3,)),
        pltpu.VMEM((2 * OWN, HID), bf16),
        pltpu.VMEM((8, 128), f32),
        pltpu.VMEM((ROWS - 1, 8, 128), f32),
        pltpu.VMEM((1, FEAT), f32),
        pltpu.VMEM((1, FEAT), f32),
        pltpu.VMEM((1, HID), f32),
        pltpu.VMEM((n, TOK, FEAT), bf16),
        pltpu.VMEM((n, TOK, 128), f32),
        pltpu.VMEM((n, TOK, FEAT), bf16),
        pltpu.VMEM((DEPTH, RANK, UPB), f32),
        pltpu.VMEM((DEPTH, RANK, DNB), f32),
        pltpu.VMEM((4 * RANK, FEAT), bf16),
        pltpu.VMEM((4 * RANK, FEAT), bf16),
        pltpu.VMEM((4 * RANK, HID), bf16),
        pltpu.VMEM((4 * RANK, HID), bf16),
        pltpu.VMEM((n, TOK, HID + 128), f32),
        pltpu.VMEM((n, TOK, 4 * RANK), bf16),
        pltpu.VMEM((n, 6, STEP, HID + 128), bf16),
        pltpu.VMEM((n, 6, STEP, HID + 128), bf16),
        pltpu.VMEM((n, TOK, HID), bf16),
        pltpu.VMEM((n, TOK, FEAT), f32),
        pltpu.VMEM((LAST, YS - 1, RING, FEAT + 128), bf16),
        pltpu.VMEM((LAST, YS - 1, RING, FEAT + 128), bf16),
        pltpu.VMEM((LAST, STEP, FEAT + 128), bf16),
        pltpu.VMEM((LAST, STEP, FEAT + 128), bf16),
        pltpu.VMEM((LAST, STEP, FEAT), f32),
        pltpu.VMEM((LAST, STEP, 128), f32),
        pltpu.VMEM((LAST, ROWS - 1, STEP, 128), f32),
        pltpu.VMEM((2, COLS - 1, STEP, HALF + 128), bf16),
        pltpu.VMEM((2, COLS - 1, STEP, HALF + 128), bf16),
        pltpu.VMEM((8, 128), f32),
        pltpu.VMEM((ROWS - 1, 8, 128), f32),
        pltpu.VMEM((8, 128), f32),
        pltpu.VMEM((COLS - 1, 8, 128), f32),
        pltpu.VMEM((TOK, 128), f32),
        pltpu.VMEM((n, RING, 128), f32),
        pltpu.VMEM((RANK, FEAT), f32),
        pltpu.VMEM((DEPTH, RANK, UPB), f32),
        pltpu.VMEM((DEPTH, RANK, UPB), f32),
        pltpu.VMEM((DEPTH, RANK, DNB), f32),
        pltpu.VMEM((DEPTH, RANK, DNB), f32),
        pltpu.VMEM((ROWS, RANK, UPB), f32),
        pltpu.VMEM((COLS, RANK, DNB), f32),
        dma((2, ROWS)),
        dma((2, 2, COLS)),
        dma((2, n)),
        dma((2, n, YS)),
        dma((2, n, YS)),
        dma((2, DEPTH)),
        dma((2, DEPTH)),
        dma((2, n, 6)),
        dma((2, n, 6)),
        dma((2, LAST, YS)),
        dma((2, LAST)),
        dma((2, LAST, ROWS)),
        dma((2, 2, COLS)),
        dma((2, ROWS)),
        dma((2, COLS)),
        dma((2, DEPTH)),
        dma((2, DEPTH)),
        dma((2, ROWS)),
        dma((2, COLS)),
    ]
    outs = pl.pallas_call(
        kernel,
        out_shape=(
            jax.ShapeDtypeStruct((2 * OWN, HID), bf16),
            jax.ShapeDtypeStruct((OWN, FEAT), bf16),
            small,
            wide,
        ),
        in_specs=[vmem, hbm] + [vmem] * 5 + [hbm],
        out_specs=(hbm,) + (vmem,) * 3,
        scratch_shapes=scratch,
        compiler_params=pltpu.CompilerParams(
            collective_id=0, has_side_effects=True, vmem_limit_bytes=56 * 1024 * 1024
        ),
        cost_estimate=pl.CostEstimate(
            flops=4 * 512 * FEAT * HID, bytes_accessed=14000000, transcendentals=10000000
        ),
        name="fused_step",
    )(tok, w, bias, gain, shift, down_w, up_w, cot)
    return pl.pallas_call(
        update_kernel,
        out_shape=(
            jax.ShapeDtypeStruct((2 * OWN, HID), bf16),
            jax.ShapeDtypeStruct((OWN, FEAT), bf16),
            small,
            small,
            small,
            wide,
            wide,
            wide,
        ),
        in_specs=[vmem] * 10,
        out_specs=(hbm, hbm) + (vmem,) * 6,
        scratch_shapes=[dma((2,))],
        name="adapter_update",
    )(*outs, down_w, up_w, down_m, down_s, up_m, up_s)


def solution(mesh):
    down = P(None, ("row", "depth"))
    up = P(None, ("col", "depth"))
    return jax.shard_map(
        shards,
        mesh=mesh,
        in_specs=(
            P(("depth", "col"), "row"),
            P("row", "col"),
            P("col"),
            P("row"),
            P("row"),
            down,
            up,
            down,
            down,
            up,
            up,
            P(("depth", "row"), "col"),
        ),
        out_specs=(
            P(("depth", "row"), "col"),
            P(("depth", "col"), "row"),
            down,
            down,
            down,
            up,
            up,
            up,
        ),
        check_vma=False,
    )
```

```python
import functools
import jax
import jax.numpy as jnp
from jax import lax
from jax.experimental import pallas as pl
from jax.experimental.pallas import tpu as pltpu
from jax.sharding import PartitionSpec as P

adapter_scale = 0.5
norm_epsilon = 1e-05
beta_first = 0.9
beta_second = 0.999
adam_step = 10
learn_rate = 0.01
decay_rate = 0.1
adam_epsilon = 1e-08

f32 = jnp.float32
bf16 = jnp.bfloat16
MESH = pl.DeviceIdType.MESH
NT = (((1,), (1,)), ((), ()))

ROWS, COLS, DEPTH = 4, 8, 8
YS = COLS // 2
CHUNKS = 4
OWN = 64
STEP = OWN // CHUNKS
TOK = STEP * COLS
FEAT, HID, RANK = 1536, 3072, 32
UPB, DNB = HID // DEPTH, FEAT // DEPTH
RING = 2 * STEP
CODE_SPAN = 120.0
LN2 = 0.6931471805599453
TILE = 512
WIDE = 1024
LAST = CHUNKS - 1


def gelu_both(v):
    inner = 0.7978845608 * (v + 0.044715 * v * v * v)
    tangent = jnp.tanh(inner)
    value = 0.5 * v * (1.0 + tangent)
    slope = 0.5 * (1.0 + tangent) + 0.5 * v * (1.0 - tangent * tangent) * 0.7978845608 * (
        1.0 + 3.0 * 0.044715 * v * v
    )
    return value, slope


def adam(weight, moment, square, gradient):
    new_moment = beta_first * moment + (1.0 - beta_first) * gradient
    new_square = beta_second * square + (1.0 - beta_second) * gradient * gradient
    update = (
        new_moment
        / (1.0 - beta_first**adam_step)
        / (jnp.sqrt(new_square / (1.0 - beta_second**adam_step)) + adam_epsilon)
    )
    return weight - learn_rate * (update + decay_rate * weight), new_moment, new_square


def encode(load, store, rows, width):
    top = jnp.zeros((rows, 1), f32)
    for t in range(0, width, TILE):
        top = jnp.maximum(top, jnp.max(jnp.abs(load(t)), axis=1, keepdims=True))
    top = (jnp.maximum(top, 1e-30) * 1.01).astype(bf16)
    factor = CODE_SPAN / top.astype(f32)
    for t in range(0, width, TILE):
        store(t, TILE, jnp.exp2(load(t) * factor).astype(bf16))
    store(width, 128, jnp.broadcast_to(top, (rows, 128)))


def decoder(load, width):
    scale = load(width, 128)[:, 0:1].astype(f32) * (1.0 / (CODE_SPAN * LN2))
    return lambda t: jnp.log(load(t, TILE).astype(f32)) * scale


def kernel(
    tok,
    w_hbm,
    bias,
    gain,
    shift,
    down_w,
    up_w,
    cot_hbm,
    hidden,
    input_grad,
    down_grad,
    up_grad,
    w,
    cot,
    local_sem,
    hid,
    stat_s,
    stat_r,
    gain_row,
    shift_row,
    bias_row,
    raw,
    mst,
    nrm,
    upg,
    dng,
    d_low,
    d_prod,
    u_low,
    u_prod,
    part,
    low,
    rs_s,
    rs_r,
    slg,
    back,
    cs_s,
    cs_r,
    lo_s,
    lo_r,
    ng,
    gst_s,
    gst_r,
    xs_s,
    xs_r,
    sst_s,
    sst_r,
    sct_s,
    sct_r,
    stt,
    low_own,
    dn_acc,
    ugs,
    ugr,
    dgs,
    dgr,
    upx,
    dnx,
    stat_sem,
    mst_sem,
    nlo_sem,
    nown_sem,
    nfwd_sem,
    upg_sem,
    dng_sem,
    rs_sem,
    ag_sem,
    cs_sem,
    lo_sem,
    gst_sem,
    xs_sem,
    sst_sem,
    sct_sem,
    ug_sem,
    dg_sem,
    ux_sem,
    dx_sem,
):
    r = lax.axis_index("row")
    c = lax.axis_index("col")
    d = lax.axis_index("depth")
    y, lo = c // 2, c % 2
    right, left, opp = (r + 1) % ROWS, (r + 3) % ROWS, (r + 2) % ROWS
    pc = y * 2 + (1 - lo)

    def remote(src, dst, sems, index, device):
        return pltpu.make_async_remote_copy(
            src_ref=src,
            dst_ref=dst,
            send_sem=sems.at[(0,) + index],
            recv_sem=sems.at[(1,) + index],
            device_id=device,
            device_id_type=MESH,
        )

    w_copy = pltpu.make_async_copy(w_hbm, w, local_sem.at[0])
    cot_copy = pltpu.make_async_copy(cot_hbm, cot, local_sem.at[1])
    hid_copy = pltpu.make_async_copy(hid, hidden, local_sem.at[2])
    w_copy.start()
    cot_copy.start()

    barrier = pltpu.get_barrier_semaphore()
    for j in range(1, ROWS):
        pl.semaphore_signal(barrier, inc=1, device_id={"row": (r + j) % ROWS}, device_id_type=MESH)
    for j in range(1, COLS):
        pl.semaphore_signal(barrier, inc=1, device_id={"col": (c + j) % COLS}, device_id_type=MESH)
    for j in range(1, DEPTH):
        pl.semaphore_signal(
            barrier, inc=1, device_id={"depth": (d + j) % DEPTH}, device_id_type=MESH
        )

    x = tok[...].astype(f32)
    lane = lax.broadcasted_iota(jnp.int32, (OWN, 128), 1)
    s1 = jnp.sum(x, axis=1, keepdims=True)
    s2 = jnp.sum(x * x, axis=1, keepdims=True)
    sums = jnp.where(lane == 0, s1, jnp.where(lane == 1, s2, 0.0))
    stat_s[...] = jnp.concatenate([sums, jnp.zeros_like(sums)], axis=0).T[0:8]
    upg[d] = up_w[...]
    dng[d] = down_w[...]
    for k in range(CHUNKS):
        raw[k, pl.ds(pl.multiple_of(STEP * c, STEP), STEP), :] = tok[STEP * k : STEP * (k + 1), :]
    pl.semaphore_wait(barrier, ROWS + COLS + DEPTH - 3)

    def stat_copy(j):
        return remote(stat_s, stat_r.at[j - 1], stat_sem, (j,), {"row": (r + j) % ROWS})

    def upg_copy(j, owner):
        return remote(upg.at[owner], upg.at[owner], upg_sem, (j,), {"depth": (d + j) % DEPTH})

    def dng_copy(j, owner):
        return remote(dng.at[owner], dng.at[owner], dng_sem, (j,), {"depth": (d + j) % DEPTH})

    for j in range(1, ROWS):
        stat_copy(j).start()

    def token_rows(k, col):
        return raw.at[k, pl.ds(pl.multiple_of(STEP * col, STEP), STEP)]

    def nlo_copy(k, col):
        return remote(token_rows(k, col), token_rows(k, col), nlo_sem, (k,), {"col": pc})

    def y_peer(j):
        return {"col": ((y + j) % YS) * 2 + lo}

    def nown_copy(k, j, col):
        return remote(token_rows(k, col), token_rows(k, col), nown_sem, (k, j), y_peer(j))

    def nfwd_copy(k, j, col):
        return remote(token_rows(k, col), token_rows(k, col), nfwd_sem, (k, j), y_peer(j))

    def ndiag_copy(j):
        peer = {"col": ((y + j) % YS) * 2 + (1 - lo)}
        return remote(token_rows(0, c), token_rows(0, c), nfwd_sem, (0, j), peer)

    for j in range(1, YS):
        ndiag_copy(j).start()
        nown_copy(0, j, c).start()

    nlo_copy(0, c).start()
    for j in range(1, DEPTH):
        dng_copy(j, d).start()
    for j in range(1, DEPTH):
        upg_copy(j, d).start()

    def forward_tokens(k):
        nlo_copy(k, pc).wait_recv()
        for j in range(1, YS):
            nfwd_copy(k, j, pc).start()

    gain_row[...] = gain[...].astype(f32).reshape(1, FEAT)
    shift_row[...] = shift[...].astype(f32).reshape(1, FEAT)
    bias_row[...] = bias[...].astype(f32).reshape(1, HID)
    for j in range(1, ROWS):
        stat_copy(j).wait_recv()
    total = stat_s[...] + stat_r[0] + stat_r[1] + stat_r[2]
    total = jnp.concatenate([total, jnp.zeros((120, 128), f32)], axis=0).T[0:OWN]
    count = 1.0 / (FEAT * ROWS)
    mean = total[:, 0:1] * count
    inv = lax.rsqrt(total[:, 1:2] * count - mean * mean + norm_epsilon)
    both = jnp.where(lane == 0, mean, inv)
    for k in range(CHUNKS):
        mst[k, pl.ds(pl.multiple_of(STEP * c, STEP), STEP), :] = both[STEP * k : STEP * (k + 1)]

    def mst_copy(late, j, col):
        rows = pl.ds(pl.multiple_of(STEP * col, STEP), STEP)
        ref = mst.at[pl.ds(1, CHUNKS - 1), rows] if late else mst.at[0, rows]
        return remote(ref, ref, mst_sem, (late, j), {"col": (c + j) % COLS})

    for late in (0, 1):
        for j in range(1, COLS):
            mst_copy(late, j, c).start()

    def send_own(k, carry):
        nlo_copy(k, c).start()
        for j in range(1, YS):
            nown_copy(k, j, c).start()
        return carry

    lax.fori_loop(1, CHUNKS, send_own, 0)

    def adapter_operands():
        for j in range(1, DEPTH):
            dng_copy(j, (d + DEPTH - j) % DEPTH).wait_recv()
        for i in range(DEPTH // 2):
            u = jnp.concatenate([dng[2 * i], dng[2 * i + 1]], axis=1)
            high = u.astype(bf16)
            mid_part = (u - high.astype(f32)).astype(bf16)
            zero = jnp.zeros_like(high)
            cols = slice(2 * DNB * i, 2 * DNB * (i + 1))
            d_low[:, cols] = jnp.concatenate([high, high, high, zero], axis=0)
            d_prod[:, cols] = jnp.concatenate([high, mid_part, high, zero], axis=0)
        for j in range(1, DEPTH):
            upg_copy(j, (d + DEPTH - j) % DEPTH).wait_recv()
        for i in range(DEPTH):
            u = upg[i]
            high = u.astype(bf16)
            mid_part = (u - high.astype(f32)).astype(bf16)
            zero = jnp.zeros_like(high)
            cols = slice(UPB * i, UPB * (i + 1))
            u_low[:, cols] = jnp.concatenate([high, high, high, zero], axis=0)
            u_prod[:, cols] = jnp.concatenate([high, mid_part, high, zero], axis=0)

    dn_acc[...] = jnp.zeros_like(dn_acc)
    w_copy.wait()
    cot_copy.wait()

    def split(value):
        high = value.astype(bf16).astype(f32)
        lanes = lax.broadcasted_iota(jnp.int32, value.shape, 1)
        return jnp.where(lanes < 2 * RANK, high, value - high).astype(bf16)

    def part_rows(k, owner, half):
        start = pl.multiple_of(RING * owner + STEP * half, STEP)
        return k, pl.ds(start, STEP)

    def rs_copy(k, slot):
        target = right if slot < 3 else left
        return remote(rs_s.at[k, slot], rs_r.at[k, slot], rs_sem, (k, slot), {"row": target})

    tail = lax.broadcasted_iota(jnp.int32, (STEP, 128), 1)

    def rs_decoder(k, slot):
        last = rs_r[k, slot, :, HID : HID + 128].astype(f32) * 1.0
        main = decoder(
            lambda t, n: last[:, 64:128] if t == HID else rs_r[k, slot, :, t : t + n], HID
        )
        scale = last[:, 96:97] * (1.0 / (CODE_SPAN * LN2))
        return main, jnp.where(tail < 2 * RANK, jnp.log(last) * scale, 0.0)

    def rs_send(k, slot, owner, half):
        kk, rows = part_rows(k, owner, half)
        value = part[kk, rows, HID : HID + 128]
        top = jnp.max(jnp.abs(value), axis=1, keepdims=True)
        top = (jnp.maximum(top, 1e-30) * 1.01).astype(bf16).astype(f32)
        code = jnp.exp2(value * (CODE_SPAN / top))

        def store(t, n, coded):
            if t == HID:
                scale = jnp.where(tail < 3 * RANK, coded.astype(f32), top)
                coded = jnp.where(tail < 2 * RANK, code, scale).astype(bf16)
            rs_s[k, slot, :, t : t + n] = coded

        encode(lambda t: part[kk, rows, t : t + TILE], store, STEP, HID)
        rs_copy(k, slot).start()

    def phase_forward(k):
        @pl.when(k == 0)
        def _():
            nlo_copy(0, pc).wait_recv()
            for j in range(1, COLS):
                mst_copy(0, j, (c + COLS - j) % COLS).wait_recv()

        @pl.when(k == 1)
        def _():
            for j in range(1, COLS):
                mst_copy(1, j, (c + COLS - j) % COLS).wait_recv()

        for j in range(1, YS):
            source = (y + YS - j) % YS
            nown_copy(k, j, source * 2 + lo).wait_recv()
            nfwd_copy(k, j, source * 2 + (1 - lo)).wait_recv()
        mean_, inv_ = mst[k, :, 0:1], mst[k, :, 1:2]
        for t in range(0, FEAT, TILE):
            cols = slice(t, t + TILE)
            nrm[k, :, cols] = (
                (raw[k, :, cols].astype(f32) - mean_) * inv_ * gain_row[:, cols]
                + shift_row[:, cols]
            ).astype(bf16)
        def rank_product():
            value = adapter_scale * lax.dot_general(
                nrm[k], d_low[...], NT, preferred_element_type=f32
            )
            part[k, :, HID : HID + 128] = value
            low[k] = split(value)

        def rank_tile(cols):
            return jnp.dot(low[k], u_prod[:, cols], preferred_element_type=f32)

        def columns(t):
            return pl.ds(pl.multiple_of(t * WIDE, WIDE), WIDE)

        def main_tile(cols):
            return jnp.dot(nrm[k], w[:, cols], preferred_element_type=f32)

        @pl.when(k == 0)
        def _():
            def tile(t, carry):
                part[k, :, columns(t)] = main_tile(columns(t))
                return carry

            def add(t, carry):
                part[k, :, columns(t)] += rank_tile(columns(t))
                return carry

            lax.fori_loop(0, HID // WIDE, tile, 0)
            adapter_operands()
            rank_product()
            lax.fori_loop(0, HID // WIDE, add, 0)

        @pl.when(k > 0)
        def _():
            def tile(t, carry):
                part[k, :, columns(t)] = main_tile(columns(t)) + rank_tile(columns(t))
                return carry

            rank_product()
            lax.fori_loop(0, HID // WIDE, tile, 0)

        rs_send(k, 0, opp, 0)
        rs_send(k, 3, opp, 1)
        rs_send(k, 1, right, 1)
        rs_send(k, 4, left, 0)

    def phase_relay(k):
        for slot, owner, half in ((0, right, 0), (3, left, 1)):
            rs_copy(k, slot).wait_recv()
            kk, rows = part_rows(k, owner, half)
            got, low_got = rs_decoder(k, slot)
            part[kk, rows, HID : HID + 128] += low_got
            for t in range(0, HID, TILE):
                part[kk, rows, t : t + TILE] += got(t)
            rs_send(k, slot + 2, owner, half)

    def slope_rows(k, owner, first, count_):
        return slg.at[k, pl.ds(pl.multiple_of(RING * owner + first, STEP), count_)]

    ag_half = (0, 1, 0, 1, 0, 1)

    def ag_copy(k, slot, owner):
        rows = slope_rows(k, owner, STEP * ag_half[slot], STEP)
        target = right if slot < 3 else left
        return remote(rows, rows, ag_sem, (k, slot), {"row": target})

    def phase_middle(k):
        for half, first, second in ((0, 4, 2), (1, 1, 5)):
            rs_copy(k, first).wait_recv()
            rs_copy(k, second).wait_recv()
            kk, rows = part_rows(k, r, half)
            (one, low_one), (two, low_two) = rs_decoder(k, first), rs_decoder(k, second)
            low_own[k, STEP * half : STEP * (half + 1), :] = (
                part[kk, rows, HID : HID + 128] + low_one + low_two
            )
            start = pl.multiple_of(OWN * half + STEP * k, STEP)
            for t in range(0, HID, TILE):
                cols = slice(t, t + TILE)
                v = part[kk, rows, cols] + one(t) + two(t) + bias_row[:, cols]
                value, slope = gelu_both(v)
                hid[pl.ds(start, STEP), cols] = value.astype(bf16)
                slg[kk, rows, cols] = (
                    cot[pl.ds(start, STEP), cols].astype(f32) * slope
                ).astype(bf16)
            for slot in (0,) if half == 0 else (3, 1, 4):
                ag_copy(k, slot, r).start()

    def phase_spread(k):
        ag_copy(k, 0, left).wait_recv()
        ag_copy(k, 2, left).start()
        ag_copy(k, 3, right).wait_recv()
        ag_copy(k, 5, right).start()

    def cs_copy(k, j):
        return remote(cs_s.at[k, j - 1], cs_r.at[k, j - 1], cs_sem, (k, j), y_peer(j))

    def ug_copy(j):
        peer = (d + j) % DEPTH
        return remote(ugs.at[peer], ugr.at[j], ug_sem, (j,), {"depth": peer})

    def dg_copy(j):
        peer = (d + j) % DEPTH
        return remote(dgs.at[peer], dgr.at[j], dg_sem, (j,), {"depth": peer})

    def ux_copy(j, owner):
        return remote(upx.at[owner], upx.at[owner], ux_sem, (j,), {"row": (r + j) % ROWS})

    def dx_copy(j, owner):
        return remote(dnx.at[owner], dnx.at[owner], dx_sem, (j,), {"col": (c + j) % COLS})

    def down_send():
        for i in range(DEPTH):
            dgs[i] = dn_acc[:, DNB * i : DNB * (i + 1)]
        for j in range(1, DEPTH):
            dg_copy(j).start()

    def up_send():
        hid_copy.start()
        lanes = lax.broadcasted_iota(jnp.int32, (RING, 128), 1)
        sides = []
        for k in range(CHUNKS):
            value = low_own[k]
            high = value.astype(bf16).astype(f32)
            both_parts = jnp.where(
                lanes < RANK, high, jnp.where(lanes < 2 * RANK, value - high, 0.0)
            )
            sides.append(both_parts.T.astype(bf16))
        for i in range(DEPTH):
            cols = slice(UPB * i, UPB * (i + 1))
            g = jnp.zeros((128, UPB), f32)
            for k in range(CHUNKS):
                rows = pl.ds(pl.multiple_of(RING * r, RING), RING)
                g += jnp.dot(sides[k], slg[k, rows, cols], preferred_element_type=f32)
            ugs[i] = g[0:RANK] + g[RANK : 2 * RANK]
        for j in range(1, DEPTH):
            ug_copy(j).start()

    def phase_backward(k):
        ag_copy(k, 1, left).wait_recv()
        ag_copy(k, 4, right).wait_recv()
        ag_copy(k, 2, opp).wait_recv()
        ag_copy(k, 5, opp).wait_recv()

        @pl.when(k == LAST)
        def _():
            for j in range(1, ROWS):
                ux_copy(j, r).start()

        slopes = slg[k]
        rank = split(
            adapter_scale * lax.dot_general(slopes, u_low[...], NT, preferred_element_type=f32)
        )
        rank_t = rank.astype(f32).T.astype(bf16)

        def grow_down(t, carry):
            cols = pl.ds(pl.multiple_of(t * TILE, TILE), TILE)
            g = jnp.dot(rank_t, nrm[k, :, cols], preferred_element_type=f32)
            dn_acc[:, cols] += g[0:RANK] + g[2 * RANK : 3 * RANK]
            return carry

        lax.fori_loop(0, FEAT // TILE, grow_down, 0)

        @pl.when(k == CHUNKS - 1)
        def _():
            down_send()

        bsize = 768

        def tile(t, carry):
            rows = pl.ds(pl.multiple_of(t * bsize, bsize), bsize)
            back[k, :, rows] = lax.dot_general(
                slg[k], w[rows, :], NT, preferred_element_type=f32
            ) + jnp.dot(rank, d_prod[:, rows], preferred_element_type=f32)
            return carry

        lax.fori_loop(0, FEAT // bsize, tile, 0)
        pl.when(k < LAST)(lambda: fold_send(k))
        pl.when(k == LAST)(last_send)

    def fold_send(k):
        for j in range(1, YS):
            rows = pl.ds(pl.multiple_of(RING * ((y + j) % YS), RING), RING)

            def store(t, n, value):
                cs_s[k, j - 1, :, t : t + n] = value

            encode(lambda t: back[k, rows, t : t + TILE], store, RING, FEAT)
            cs_copy(k, j).start()

    def xs_copy(j):
        return remote(xs_s.at[j - 1], xs_r.at[j - 1], xs_sem, (j,), {"col": (c + j) % COLS})

    def sst_copy(j):
        return remote(sst_s, sst_r.at[j - 1], sst_sem, (j,), {"row": (r + j) % ROWS})

    def sct_copy(j):
        return remote(sct_s, sct_r.at[j - 1], sct_sem, (j,), {"col": (c + j) % COLS})

    def last_send():
        for j in range(1, COLS):
            rows = pl.ds(pl.multiple_of(STEP * ((c + j) % COLS), STEP), STEP)

            def store(t, n, value):
                xs_s[j - 1, :, t : t + n] = value

            encode(lambda t: back[LAST, rows, t : t + TILE], store, STEP, FEAT)
            xs_copy(j).start()
        mean_, inv_ = mst[LAST, :, 0:1], mst[LAST, :, 1:2]
        one = jnp.zeros((TOK, 1), f32)
        two = jnp.zeros((TOK, 1), f32)
        for t in range(0, FEAT, 256):
            cols = slice(t, t + 256)
            scaled = back[LAST, :, cols] * gain_row[:, cols]
            centred = (raw[LAST, :, cols].astype(f32) - mean_) * inv_
            one += jnp.sum(scaled, axis=1, keepdims=True)
            two += jnp.sum(scaled * centred, axis=1, keepdims=True)
        lanes = lax.broadcasted_iota(jnp.int32, (TOK, 128), 1)
        sst_s[...] = jnp.where(lanes == 0, one, jnp.where(lanes == 1, two, 0.0)).T[0:8]
        for j in range(1, ROWS):
            sst_copy(j).start()

    def last_stats():
        for j in range(1, ROWS):
            sst_copy(j).wait_recv()
        sct_s[...] = sst_s[...] + sst_r[0] + sst_r[1] + sst_r[2]
        for j in range(1, COLS):
            sct_copy(j).start()

    def last_finish():
        for j in range(1, COLS):
            sct_copy(j).wait_recv()
        sums_ = sct_s[...]
        for j in range(1, COLS):
            sums_ += sct_r[j - 1]
        stt[...] = (jnp.concatenate([sums_, jnp.zeros((120, 128), f32)], axis=0) * count).T
        mine = pl.ds(pl.multiple_of(STEP * c, STEP), STEP)
        one, two = stt[mine, 0:1], stt[mine, 1:2]
        inv_ = mst[LAST, mine, 1:2]
        for j in range(1, COLS):
            xs_copy(j).wait_recv()
        got = [
            decoder(lambda t, n, j=j: xs_r[j - 1, :, t : t + n], FEAT) for j in range(1, COLS)
        ]
        for t in range(0, FEAT, TILE):
            cols = slice(t, t + TILE)
            value = back[LAST, mine, cols]
            for part_ in got:
                value += part_(t)
            input_grad[STEP * LAST : STEP * CHUNKS, cols] = (
                inv_ * (value * gain_row[:, cols] - one - own_centred(LAST, cols) * two)
            ).astype(bf16)

    def lo_copy(k):
        return remote(lo_s.at[k], lo_r.at[k], lo_sem, (k,), {"col": pc})

    def phase_fold(k):
        mine = pl.ds(pl.multiple_of(RING * y, RING), RING)
        for j in range(1, YS):
            cs_copy(k, j).wait_recv()
            got = decoder(lambda t, n: cs_r[k, j - 1, :, t : t + n], FEAT)
            for t in range(0, FEAT, TILE):
                back[k, mine, t : t + TILE] += got(t)
        other = pl.ds(pl.multiple_of(RING * y + STEP * (1 - lo), STEP), STEP)

        def store(t, n, value):
            lo_s[k, :, t : t + n] = value

        encode(lambda t: back[k, other, t : t + TILE], store, STEP, FEAT)
        lo_copy(k).start()

    def gst_copy(k, j):
        return remote(gst_s.at[k], gst_r.at[k, j - 1], gst_sem, (k, j), {"row": (r + j) % ROWS})

    def own_rows(k):
        return pl.ds(pl.multiple_of(STEP * k, STEP), STEP)

    def own_centred(k, cols):
        rows = pl.ds(pl.multiple_of(STEP * c, STEP), STEP)
        return (tok[own_rows(k), cols].astype(f32) - mst[k, rows, 0:1]) * mst[k, rows, 1:2]

    def phase_stats(k):
        lo_copy(k).wait_recv()
        mine = pl.ds(pl.multiple_of(RING * y + STEP * lo, STEP), STEP)
        got = decoder(lambda t, n: lo_r[k, :, t : t + n], FEAT)
        one = jnp.zeros((STEP, 1), f32)
        two = jnp.zeros((STEP, 1), f32)
        for t in range(0, FEAT, TILE):
            cols = slice(t, t + TILE)
            scaled = (back[k, mine, cols] + got(t)) * gain_row[:, cols]
            ng[k, :, cols] = scaled
            one += jnp.sum(scaled, axis=1, keepdims=True)
            two += jnp.sum(scaled * own_centred(k, cols), axis=1, keepdims=True)
        lanes = lax.broadcasted_iota(jnp.int32, (STEP, 128), 1)
        gst_s[k] = jnp.where(lanes == 0, one, jnp.where(lanes == 1, two, 0.0))
        for j in range(1, ROWS):
            gst_copy(k, j).start()

    def phase_finish(k):
        for j in range(1, ROWS):
            gst_copy(k, j).wait_recv()
        sums = (gst_s[k] + gst_r[k, 0] + gst_r[k, 1] + gst_r[k, 2]) * count
        inv_ = mst[k, pl.ds(pl.multiple_of(STEP * c, STEP), STEP), 1:2]
        for t in range(0, FEAT, TILE):
            cols = slice(t, t + TILE)
            input_grad[own_rows(k), cols] = (
                inv_ * (ng[k, :, cols] - sums[:, 0:1] - own_centred(k, cols) * sums[:, 1:2])
            ).astype(bf16)

    def up_sum():
        total_ = ugs[d]
        for j in range(1, DEPTH):
            ug_copy(j).wait_recv()
            total_ += ugr[j]
        upx[r] = total_

    def grads_spread():
        dn_sum = dgs[d]
        for j in range(1, DEPTH):
            dg_copy(j).wait_recv()
            dn_sum += dgr[j]
        dnx[c] = dn_sum
        for j in range(1, COLS):
            dx_copy(j, c).start()

    def drain_early():
        for j in range(1, ROWS):
            stat_copy(j).wait_send()
        for j in range(1, COLS):
            mst_copy(0, j, c).wait_send()
            mst_copy(1, j, c).wait_send()
        for j in range(1, DEPTH):
            dng_copy(j, d).wait_send()
            upg_copy(j, d).wait_send()
        for j in range(1, YS):
            ndiag_copy(j).wait_send()

        def drain_tokens(k, carry):
            for j in range(1, YS):
                nfwd_copy(k, j, pc).wait_send()
            return carry

        def drain(k, carry):
            nlo_copy(k, c).wait_send()
            for j in range(1, YS):
                nown_copy(k, j, c).wait_send()
            for slot in range(6):
                rs_copy(k, slot).wait_send()
            return carry

        lax.fori_loop(0, CHUNKS, drain, 0)
        lax.fori_loop(1, CHUNKS, drain_tokens, 0)

    def iteration(it, carry):
        def step(condition, run):
            pl.when(condition)(run)

        step(it < CHUNKS, lambda: phase_forward(it))

        @pl.when(it == 0)
        def _():
            for k in range(1, CHUNKS):
                forward_tokens(k)

        step((it >= 2) & (it < CHUNKS), lambda: phase_spread(it - 2))
        step(it < CHUNKS, lambda: phase_relay(it))
        step((it >= 1) & (it < CHUNKS + 1), lambda: phase_middle(it - 1))
        step((it >= CHUNKS) & (it < CHUNKS + 2), lambda: phase_spread(it - 2))
        step(it == CHUNKS, up_send)
        step(it == CHUNKS + 2, drain_early)
        step((it >= 3) & (it < CHUNKS + 3), lambda: phase_backward(it - 3))
        step(it == CHUNKS + 1, up_sum)
        step((it >= CHUNKS) & (it < CHUNKS + LAST), lambda: phase_fold(it - CHUNKS))
        step(it >= CHUNKS + 2, lambda: phase_finish(it - CHUNKS - 2))
        step((it > CHUNKS) & (it <= CHUNKS + LAST), lambda: phase_stats(it - CHUNKS - 1))
        step(it == CHUNKS + 2, last_stats)
        step(it == CHUNKS + 2, grads_spread)
        step(it == CHUNKS + 3, last_finish)
        return carry

    lax.fori_loop(0, CHUNKS + LAST + 2, iteration, 0)

    for j in range(1, ROWS):
        ux_copy(j, (r + ROWS - j) % ROWS).wait_recv()
    for j in range(1, COLS):
        dx_copy(j, (c + COLS - j) % COLS).wait_recv()
    up_gradient = upx[0]
    for i in range(1, ROWS):
        up_gradient += upx[i]
    down_gradient = dnx[0]
    for i in range(1, COLS):
        down_gradient += dnx[i]
    up_grad[...] = up_gradient
    down_grad[...] = down_gradient

    hid_copy.wait()
    for j in range(1, ROWS):
        ux_copy(j, r).wait_send()
    for j in range(1, COLS):
        dx_copy(j, c).wait_send()
    for j in range(1, DEPTH):
        ug_copy(j).wait_send()
        dg_copy(j).wait_send()

    def drain(k, carry):
        for j in range(1, YS):
            cs_copy(k, j).wait_send()
        lo_copy(k).wait_send()
        for j in range(1, ROWS):
            gst_copy(k, j).wait_send()
        return carry

    lax.fori_loop(0, LAST, drain, 0)

    def drain_slopes(k, carry):
        for slot, owner in ((0, r), (1, r), (2, left), (3, r), (4, r), (5, right)):
            ag_copy(k, slot, owner).wait_send()
        return carry

    lax.fori_loop(0, CHUNKS, drain_slopes, 0)
    for j in range(1, ROWS):
        sst_copy(j).wait_send()
    for j in range(1, COLS):
        xs_copy(j).wait_send()
        sct_copy(j).wait_send()


def update_kernel(
    hidden,
    input_grad,
    down_grad,
    up_grad,
    down_w,
    up_w,
    down_m,
    down_s,
    up_m,
    up_s,
    hidden_out,
    input_grad_out,
    new_down_w,
    new_down_m,
    new_down_s,
    new_up_w,
    new_up_m,
    new_up_s,
    sems,
):
    copies = (
        pltpu.make_async_copy(hidden, hidden_out, sems.at[0]),
        pltpu.make_async_copy(input_grad, input_grad_out, sems.at[1]),
    )
    for copy in copies:
        copy.start()
    new_up_w[...], new_up_m[...], new_up_s[...] = adam(
        up_w[...], up_m[...], up_s[...], up_grad[...]
    )
    new_down_w[...], new_down_m[...], new_down_s[...] = adam(
        down_w[...], down_m[...], down_s[...], down_grad[...]
    )
    for copy in copies:
        copy.wait()


def shards(*blocks):
    (tok, w, bias, gain, shift, down_w, up_w, down_m, down_s, up_m, up_s, cot) = blocks
    vmem = pl.BlockSpec(memory_space=pltpu.VMEM)
    hbm = pl.BlockSpec(memory_space=pl.ANY)
    n = CHUNKS
    dma = pltpu.SemaphoreType.DMA
    small = jax.ShapeDtypeStruct((RANK, DNB), f32)
    wide = jax.ShapeDtypeStruct((RANK, UPB), f32)
    scratch = [
        pltpu.VMEM((FEAT, HID), bf16),
        pltpu.VMEM((2 * OWN, HID), bf16),
        dma((3,)),
        pltpu.VMEM((2 * OWN, HID), bf16),
        pltpu.VMEM((8, 128), f32),
        pltpu.VMEM((ROWS - 1, 8, 128), f32),
        pltpu.VMEM((1, FEAT), f32),
        pltpu.VMEM((1, FEAT), f32),
        pltpu.VMEM((1, HID), f32),
        pltpu.VMEM((n, TOK, FEAT), bf16),
        pltpu.VMEM((n, TOK, 128), f32),
        pltpu.VMEM((n, TOK, FEAT), bf16),
        pltpu.VMEM((DEPTH, RANK, UPB), f32),
        pltpu.VMEM((DEPTH, RANK, DNB), f32),
        pltpu.VMEM((4 * RANK, FEAT), bf16),
        pltpu.VMEM((4 * RANK, FEAT), bf16),
        pltpu.VMEM((4 * RANK, HID), bf16),
        pltpu.VMEM((4 * RANK, HID), bf16),
        pltpu.VMEM((n, TOK, HID + 128), f32),
        pltpu.VMEM((n, TOK, 4 * RANK), bf16),
        pltpu.VMEM((n, 6, STEP, HID + 128), bf16),
        pltpu.VMEM((n, 6, STEP, HID + 128), bf16),
        pltpu.VMEM((n, TOK, HID), bf16),
        pltpu.VMEM((n, TOK, FEAT), f32),
        pltpu.VMEM((LAST, YS - 1, RING, FEAT + 128), bf16),
        pltpu.VMEM((LAST, YS - 1, RING, FEAT + 128), bf16),
        pltpu.VMEM((LAST, STEP, FEAT + 128), bf16),
        pltpu.VMEM((LAST, STEP, FEAT + 128), bf16),
        pltpu.VMEM((LAST, STEP, FEAT), f32),
        pltpu.VMEM((LAST, STEP, 128), f32),
        pltpu.VMEM((LAST, ROWS - 1, STEP, 128), f32),
        pltpu.VMEM((COLS - 1, STEP, FEAT + 128), bf16),
        pltpu.VMEM((COLS - 1, STEP, FEAT + 128), bf16),
        pltpu.VMEM((8, 128), f32),
        pltpu.VMEM((ROWS - 1, 8, 128), f32),
        pltpu.VMEM((8, 128), f32),
        pltpu.VMEM((COLS - 1, 8, 128), f32),
        pltpu.VMEM((TOK, 128), f32),
        pltpu.VMEM((n, RING, 128), f32),
        pltpu.VMEM((RANK, FEAT), f32),
        pltpu.VMEM((DEPTH, RANK, UPB), f32),
        pltpu.VMEM((DEPTH, RANK, UPB), f32),
        pltpu.VMEM((DEPTH, RANK, DNB), f32),
        pltpu.VMEM((DEPTH, RANK, DNB), f32),
        pltpu.VMEM((ROWS, RANK, UPB), f32),
        pltpu.VMEM((COLS, RANK, DNB), f32),
        dma((2, ROWS)),
        dma((2, 2, COLS)),
        dma((2, n)),
        dma((2, n, YS)),
        dma((2, n, YS)),
        dma((2, DEPTH)),
        dma((2, DEPTH)),
        dma((2, n, 6)),
        dma((2, n, 6)),
        dma((2, LAST, YS)),
        dma((2, LAST)),
        dma((2, LAST, ROWS)),
        dma((2, COLS)),
        dma((2, ROWS)),
        dma((2, COLS)),
        dma((2, DEPTH)),
        dma((2, DEPTH)),
        dma((2, ROWS)),
        dma((2, COLS)),
    ]
    outs = pl.pallas_call(
        kernel,
        out_shape=(
            jax.ShapeDtypeStruct((2 * OWN, HID), bf16),
            jax.ShapeDtypeStruct((OWN, FEAT), bf16),
            small,
            wide,
        ),
        in_specs=[vmem, hbm] + [vmem] * 5 + [hbm],
        out_specs=(hbm,) + (vmem,) * 3,
        scratch_shapes=scratch,
        compiler_params=pltpu.CompilerParams(
            collective_id=0, has_side_effects=True, vmem_limit_bytes=56 * 1024 * 1024
        ),
        cost_estimate=pl.CostEstimate(
            flops=4 * 512 * FEAT * HID, bytes_accessed=14000000, transcendentals=10000000
        ),
        name="fused_step",
    )(tok, w, bias, gain, shift, down_w, up_w, cot)
    return pl.pallas_call(
        update_kernel,
        out_shape=(
            jax.ShapeDtypeStruct((2 * OWN, HID), bf16),
            jax.ShapeDtypeStruct((OWN, FEAT), bf16),
            small,
            small,
            small,
            wide,
            wide,
            wide,
        ),
        in_specs=[vmem] * 10,
        out_specs=(hbm, hbm) + (vmem,) * 6,
        scratch_shapes=[dma((2,))],
        name="adapter_update",
    )(*outs, down_w, up_w, down_m, down_s, up_m, up_s)


def solution(mesh):
    down = P(None, ("row", "depth"))
    up = P(None, ("col", "depth"))
    return jax.shard_map(
        shards,
        mesh=mesh,
        in_specs=(
            P(("depth", "col"), "row"),
            P("row", "col"),
            P("col"),
            P("row"),
            P("row"),
            down,
            up,
            down,
            down,
            up,
            up,
            P(("depth", "row"), "col"),
        ),
        out_specs=(
            P(("depth", "row"), "col"),
            P(("depth", "col"), "row"),
            down,
            down,
            down,
            up,
            up,
            up,
        ),
        check_vma=False,
    )
```
